32 devices in a mesh: dp: 16 (over z, x, core), tensor: 2 (over y).
Axes of the slice: x: 2, y: 2, z: 4, core: 2. Of those that a mesh axis runs over, the one named last changes fastest.
Arguments:
- tokens: bfloat16 [16384, 768], P('dp'), may hold values from -6 to 6
- cotangent: bfloat16 [16384, 768], P('dp'), may hold values from -12 to 12
- tie_sources: int32 [12], replicated, may hold values from 0 to 1, as said below
- attn_weight: float32 [2, 768, 3, 768], P(None, 'dp', None, 'tensor'), may hold values from -0.3125 to 0.3125
- attn_momentum: float32 [2, 768, 3, 768], P(None, 'dp', None, 'tensor'), may hold values from -2048 to 2048
- attn_average: float32 [2, 768, 3, 768], P(None, 'dp', None, 'tensor'), may hold values from -0.3125 to 0.3125
- proj_weight: float32 [2, 768, 768], P(None, 'tensor', 'dp'), may hold values from -0.625 to 0.625
- proj_momentum: float32 [2, 768, 768], P(None, 'tensor', 'dp'), may hold values from -896 to 896
- proj_average: float32 [2, 768, 768], P(None, 'tensor', 'dp'), may hold values from -0.625 to 0.625
- fc_weight: float32 [2, 768, 3072], P(None, 'dp', 'tensor'), may hold values from -0.21875 to 0.21875
- fc_momentum: float32 [2, 768, 3072], P(None, 'dp', 'tensor'), may hold values from -640 to 640
- fc_average: float32 [2, 768, 3072], P(None, 'dp', 'tensor'), may hold values from -0.21875 to 0.21875
- out_weight: float32 [2, 3072, 768], P(None, 'tensor', 'dp'), may hold values from -0.15625 to 0.15625
- out_momentum: float32 [2, 3072, 768], P(None, 'tensor', 'dp'), may hold values from -896 to 896
- out_average: float32 [2, 3072, 768], P(None, 'tensor', 'dp'), may hold values from -0.15625 to 0.15625
- norm_vectors: float32 [2, 6, 768], replicated, may hold values from -1.2 to 1.5, as said below
- norm_momentum: float32 [2, 6, 768], replicated, may hold values from -224 to 224
- head_bias: float32 [2, 2, 768], P(None, None, 'tensor'), may hold values from -4 to 4
- head_bias_momentum: float32 [2, 2, 768], P(None, None, 'tensor'), may hold values from -224 to 224
- fc_bias: float32 [2, 3072], P(None, 'tensor'), may hold values from -4 to 4
- fc_bias_momentum: float32 [2, 3072], P(None, 'tensor'), may hold values from -80 to 80
Outputs:
- block_output: bfloat16 [16384, 768], P('dp')
- input_grad: bfloat16 [16384, 768], P('dp')
- new_attn_weight: float32 [2, 768, 3, 768], P(None, 'dp', None, 'tensor')
- new_attn_momentum: float32 [2, 768, 3, 768], P(None, 'dp', None, 'tensor')
- new_attn_average: float32 [2, 768, 3, 768], P(None, 'dp', None, 'tensor')
- new_proj_weight: float32 [2, 768, 768], P(None, 'tensor', 'dp')
- new_proj_momentum: float32 [2, 768, 768], P(None, 'tensor', 'dp')
- new_proj_average: float32 [2, 768, 768], P(None, 'tensor', 'dp')
- new_fc_weight: float32 [2, 768, 3072], P(None, 'dp', 'tensor')
- new_fc_momentum: float32 [2, 768, 3072], P(None, 'dp', 'tensor')
- new_fc_average: float32 [2, 768, 3072], P(None, 'dp', 'tensor')
- new_out_weight: float32 [2, 3072, 768], P(None, 'tensor', 'dp')
- new_out_momentum: float32 [2, 3072, 768], P(None, 'tensor', 'dp')
- new_out_average: float32 [2, 3072, 768], P(None, 'tensor', 'dp')
- new_norm_vectors: float32 [2, 6, 768], replicated
- new_norm_momentum: float32 [2, 6, 768], replicated
- new_head_bias: float32 [2, 2, 768], P(None, None, 'tensor')
- new_head_bias_momentum: float32 [2, 2, 768], P(None, None, 'tensor')
- new_fc_bias: float32 [2, 3072], P(None, 'tensor')
- new_fc_bias_momentum: float32 [2, 3072], P(None, 'tensor')
The draws below stay inside these ranges and needn't reach their ends.
Inputs may be any that keep to these rules, and one draw needn't show every extreme that they name: `tie_sources`: entry p names the stored set that supplies parameter p; the values 0 and 1 both occur. `norm_vectors`: rows 0 and 2 lie between 0.5 and 1.5.
All inputs are finite; a program needn't handle non-finite values.
Results may differ from the reference program's by a relative error of at most 0.033.
Values may be sent and summed in bfloat16 or wider, within the bound.
No kernel may reach another device: no remote copies, remote signals or barrier semaphores. Data moves between devices by JAX's collectives and lax.ppermute only.
A program may use at most 128 MiB of HBM per device.

```python
import math
import jax
import jax.numpy as jnp
from jax import lax

D = 768
HEADS = 12
HEAD = 64
FF = 3072
LEN = 1024
UNIQUE = 2
PARAMS = 12
NS_STEPS = 5
BLOCK = 512
TOKENS = 16384
N_TENSOR = 2


def draw_cotangent(key, part):
    key = jax.random.fold_in(key, 11)
    seq_count = TOKENS // LEN
    position = jnp.arange(TOKENS) // LEN
    fraction = position.astype(jnp.float32) / max(seq_count - 1, 1)
    base = jax.random.truncated_normal(key, -4.0, 4.0, (TOKENS, D), jnp.float32)
    rising = 1.0 + 2.0 * fraction
    return (base * rising[:, None]).astype(jnp.bfloat16)


def draw_tie_sources(key, part):
    key = jax.random.fold_in(key, 5)
    first_key, second_key = jax.random.split(key)
    others = jax.random.randint(first_key, (PARAMS - 2,), 0, UNIQUE, dtype=jnp.int32)
    ends = jnp.array([0, UNIQUE - 1], dtype=jnp.int32)
    return jax.random.permutation(second_key, jnp.concatenate([ends, others]))


def draw_norm_vectors(key, part):
    key = jax.random.fold_in(key, 7)
    gain_key, shift_key = jax.random.split(key)
    gains = jax.random.uniform(gain_key, (UNIQUE, 6, D), jnp.float32, 0.5, 1.5)
    shifts = 0.3 * jax.random.truncated_normal(shift_key, -4.0, 4.0, (UNIQUE, 6, D), jnp.float32)
    is_gain = (jnp.arange(6) == 0) | (jnp.arange(6) == 2)
    return jnp.where(is_gain[None, :, None], gains, shifts)


def steps_of(stream_key, extent, pieces, least, largest):
    gain = 1.0
    for dim, blocks in pieces:
        draws = jax.random.uniform(jax.random.fold_in(jax.random.fold_in(stream_key, 6), dim), (blocks,), jnp.float32, least / len(pieces), largest / len(pieces))
        gain = gain * jnp.repeat(jnp.exp(draws), extent[dim] // blocks).reshape((-1,) + (1,) * (len(extent) - 1 - dim))
    return gain


def gaussian(rng, extent, width, bound, cuts=(), held_as=jnp.bfloat16):
    entries = width * jax.random.normal(rng, extent, jnp.float32)
    if cuts:
        entries = entries * steps_of(rng, extent, cuts, -0.22, 0.18)
    return jnp.clip(entries, -bound, bound).astype(held_as)


def setup_inputs(seed: int = 0) -> dict:
    arg_keys = jax.random.split(jax.random.key(seed), 22)
    tokens = gaussian(arg_keys[0], (TOKENS, D), 1.0, 6.0, ((0, 16),))
    cotangent = draw_cotangent(jax.random.fold_in(arg_keys[21], 71), 0)
    tie_sources = draw_tie_sources(jax.random.fold_in(arg_keys[21], 71), 0)
    attn_weight = gaussian(arg_keys[3], (UNIQUE, D, 3, D), (D // 2) ** -0.5, 0.3125, ((1, 16), (3, 2)), jnp.float32)
    attn_momentum = gaussian(arg_keys[4], (UNIQUE, D, 3, D), (3 * TOKENS ** 0.5), 2048.0, ((1, 16), (3, 2)), jnp.float32)
    attn_average = gaussian(arg_keys[5], (UNIQUE, D, 3, D), (D // 2) ** -0.5, 0.3125, ((1, 16), (3, 2)), jnp.float32)
    proj_weight = gaussian(arg_keys[6], (UNIQUE, D, D), (D // 8) ** -0.5, 0.625, ((1, 2), (2, 16)), jnp.float32)
    proj_momentum = gaussian(arg_keys[7], (UNIQUE, D, D), (1.2 * TOKENS ** 0.5), 896.0, ((1, 2), (2, 16)), jnp.float32)
    proj_average = gaussian(arg_keys[8], (UNIQUE, D, D), (D // 8) ** -0.5, 0.625, ((1, 2), (2, 16)), jnp.float32)
    fc_weight = gaussian(arg_keys[9], (UNIQUE, D, FF), D ** -0.5, 0.21875, ((1, 16), (2, 2)), jnp.float32)
    fc_momentum = gaussian(arg_keys[10], (UNIQUE, D, FF), (0.85 * TOKENS ** 0.5), 640.0, ((1, 16), (2, 2)), jnp.float32)
    fc_average = gaussian(arg_keys[11], (UNIQUE, D, FF), D ** -0.5, 0.21875, ((1, 16), (2, 2)), jnp.float32)
    out_weight = gaussian(arg_keys[12], (UNIQUE, FF, D), (FF // 2) ** -0.5, 0.15625, ((1, 2), (2, 16)), jnp.float32)
    out_momentum = gaussian(arg_keys[13], (UNIQUE, FF, D), (1.2 * TOKENS ** 0.5), 896.0, ((1, 2), (2, 16)), jnp.float32)
    out_average = gaussian(arg_keys[14], (UNIQUE, FF, D), (FF // 2) ** -0.5, 0.15625, ((1, 2), (2, 16)), jnp.float32)
    norm_vectors = draw_norm_vectors(jax.random.fold_in(arg_keys[21], 71), 0)
    norm_momentum = gaussian(arg_keys[16], (UNIQUE, 6, D), (0.3 * TOKENS ** 0.5), 224.0, (), jnp.float32)
    head_bias = gaussian(arg_keys[17], (UNIQUE, 2, D), 0.3, 4.0, ((2, 2),), jnp.float32)
    head_bias_momentum = gaussian(arg_keys[18], (UNIQUE, 2, D), (0.3 * TOKENS ** 0.5), 224.0, ((2, 2),), jnp.float32)
    fc_bias = gaussian(arg_keys[19], (UNIQUE, FF), 0.3, 4.0, ((1, 2),), jnp.float32)
    fc_bias_momentum = gaussian(arg_keys[20], (UNIQUE, FF), (0.1 * TOKENS ** 0.5), 80.0, ((1, 2),), jnp.float32)
    return dict(tokens=tokens, cotangent=cotangent, tie_sources=tie_sources, attn_weight=attn_weight, attn_momentum=attn_momentum, attn_average=attn_average, proj_weight=proj_weight, proj_momentum=proj_momentum, proj_average=proj_average, fc_weight=fc_weight, fc_momentum=fc_momentum, fc_average=fc_average, out_weight=out_weight, out_momentum=out_momentum, out_average=out_average, norm_vectors=norm_vectors, norm_momentum=norm_momentum, head_bias=head_bias, head_bias_momentum=head_bias_momentum, fc_bias=fc_bias, fc_bias_momentum=fc_bias_momentum)


@jax.custom_vjp
def low(v):
    return lax.optimization_barrier(v.astype(jnp.bfloat16)).astype(jnp.float32)

@jax.custom_vjp
def low_back(v):
    return v

def low_keep(v):
    return (low(v), None)

def low_pass(kept, grad):
    return (grad,)

def back_keep(v):
    return (v, None)

def back_low(kept, grad):
    return (low(grad),)
low.defvjp(low_keep, low_pass)
low_back.defvjp(back_keep, back_low)
highest = lax.Precision.HIGHEST
norm_epsilon = 1e-05
gelu_scale = 0.7978845608028654
coef_one = 3.4445
coef_three = -4.775
coef_five = 2.0315
row_params = (0, 1, 6, 7, 5, 11)
vector_decay = 0.9
matrix_decay = 0.5
average_decay = 0.75

def rounded(values):
    return lax.optimization_barrier(values.astype(jnp.bfloat16)).astype(jnp.float32)

def gelu_curve(values):
    return 0.5 * values * (1.0 + jnp.tanh(gelu_scale * (values + 0.044715 * values * values * values)))

def layer_norm(values, gain_row, shift_row):
    centre = lax.optimization_barrier(jnp.mean(values, axis=-1, keepdims=True))
    centred = values - centre
    spread = lax.optimization_barrier(jnp.mean(centred * centred, axis=-1, keepdims=True))
    return centred * lax.rsqrt(spread + norm_epsilon) * gain_row + shift_row

def attention(query_rows, key_rows, value_rows):
    block_count = LEN // BLOCK
    score_scale = HEAD ** (-0.5)
    blocks = query_rows.reshape(block_count, BLOCK, HEADS, HEAD)
    keys_all = key_rows.reshape(LEN, HEADS, HEAD)
    values_all = value_rows.reshape(LEN, HEADS, HEAD)

    def one_block(inputs):
        block_query, block_index = inputs
        scores = jnp.einsum('qhd,khd->hqk', block_query, keys_all, precision=highest) * score_scale
        scores = low_back(scores)
        query_at = block_index * BLOCK + jnp.arange(BLOCK)
        allowed = jnp.arange(LEN)[None, :] <= query_at[:, None]
        scores = jnp.where(allowed[None], scores, -1e+30)
        row_max = lax.optimization_barrier(jnp.max(scores, axis=-1, keepdims=True))
        weights = jnp.exp(scores - row_max)
        probs_low = low(weights / lax.optimization_barrier(jnp.sum(weights, axis=-1, keepdims=True)))
        return jnp.einsum('hqk,khd->qhd', probs_low, values_all, precision=highest)
    attn_mixed = lax.map(jax.checkpoint(one_block), (blocks, jnp.arange(block_count)))
    return attn_mixed.reshape(LEN, HEADS * HEAD)

def forward(layer, inputs):
    attn_w, proj_w, fc_w, out_w, norm_rows, query_bias, hidden_bias = layer
    attn_in = low(layer_norm(inputs, norm_rows[0], norm_rows[1]))
    projected = jnp.dot(attn_in, low(attn_w).reshape(D, 3 * D), precision=highest)
    bias_row = jnp.concatenate([query_bias[0], jnp.zeros((D,), jnp.float32), query_bias[1]])
    triple = low(low_back(projected + bias_row))
    attn_mixed = low(low_back(attention(triple[:, :D], triple[:, D:2 * D], triple[:, 2 * D:])))
    after_attn = inputs + (low_back(jnp.dot(attn_mixed, low(proj_w), precision=highest)) + norm_rows[4])
    mlp_in = low(layer_norm(after_attn, norm_rows[2], norm_rows[3]))
    hidden_in = low_back(jnp.dot(mlp_in, low(fc_w), precision=highest) + hidden_bias)
    activated = low(gelu_curve(hidden_in))
    return after_attn + (low_back(jnp.dot(activated, low(out_w), precision=highest)) + norm_rows[5])

def sum_parts(halves):
    total = jnp.zeros((D, D), jnp.float32)
    for piece in halves:
        total = total + rounded(jnp.dot(piece, piece.T, preferred_element_type=jnp.float32))
    return total

def newton(halves):
    starts = [piece.astype(jnp.bfloat16) for piece in halves]
    total = sum_parts(starts)
    factor = lax.rsqrt(jnp.trace(total) + 1e-07)
    current = [(piece.astype(jnp.float32) * factor).astype(jnp.bfloat16) for piece in starts]
    gram_low = (total * factor * factor).astype(jnp.bfloat16)
    for round_index in range(NS_STEPS):
        if round_index > 0:
            gram_low = sum_parts(current).astype(jnp.bfloat16)
        square = jnp.dot(gram_low, gram_low, preferred_element_type=jnp.float32)
        mixing = (coef_three * gram_low.astype(jnp.float32) + coef_five * square).astype(jnp.bfloat16)
        current = [(coef_one * piece.astype(jnp.float32) + jnp.dot(mixing, piece, preferred_element_type=jnp.float32)).astype(jnp.bfloat16) for piece in current]
    return current

def split_halves(kind_index, matrix):
    head_part = D // N_TENSOR
    hidden_part = FF // N_TENSOR
    halves = []
    for part_index in range(N_TENSOR):
        if kind_index == 0:
            halves.append(matrix[:, :, part_index * head_part:(part_index + 1) * head_part].reshape(D, 3 * head_part))
        elif kind_index == 1:
            halves.append(matrix[part_index * head_part:(part_index + 1) * head_part, :].T)
        elif kind_index == 2:
            halves.append(matrix[:, part_index * hidden_part:(part_index + 1) * hidden_part])
        else:
            halves.append(matrix[part_index * hidden_part:(part_index + 1) * hidden_part, :].T)
    return halves

def join_halves(kind_index, halves):
    if kind_index == 0:
        return jnp.concatenate([piece.reshape(D, 3, -1) for piece in halves], axis=2)
    if kind_index == 2:
        return jnp.concatenate(halves, axis=1)
    return jnp.concatenate([piece.T for piece in halves], axis=0)

def reference(tokens, cotangent, tie_sources, attn_weight, attn_momentum, attn_average, proj_weight, proj_momentum, proj_average, fc_weight, fc_momentum, fc_average, out_weight, out_momentum, out_average, norm_vectors, norm_momentum, head_bias, head_bias_momentum, fc_bias, fc_bias_momentum):

    def choose_slot(bank, param_index):
        return lax.dynamic_index_in_dim(bank, tie_sources[param_index], 0, keepdims=False)
    norm_rows = jnp.stack([norm_vectors[tie_sources[param_index], row_index] for row_index, param_index in enumerate(row_params)])
    layer = (choose_slot(attn_weight, 2), choose_slot(proj_weight, 4), choose_slot(fc_weight, 8), choose_slot(out_weight, 10), norm_rows, choose_slot(head_bias, 3), choose_slot(fc_bias, 9))
    seq_count = TOKENS // LEN
    inputs = tokens.astype(jnp.float32).reshape(seq_count, LEN, D)
    grads_in = cotangent.astype(jnp.float32).reshape(seq_count, LEN, D)

    def one_sequence(totals, pair_in):
        seq_inputs, seq_grads = pair_in
        seq_outputs, pull = jax.vjp(forward, layer, seq_inputs)
        layer_grads, input_grads = pull(seq_grads)
        totals = jax.tree.map(jnp.add, totals, layer_grads)
        return (totals, (seq_outputs.astype(jnp.bfloat16), input_grads.astype(jnp.bfloat16)))
    zero_tree = jax.tree.map(jnp.zeros_like, layer)
    sums, (outputs, input_grads) = lax.scan(one_sequence, zero_tree, (inputs, grads_in))
    block_output = outputs.reshape(TOKENS, D)
    input_grad = input_grads.reshape(TOKENS, D)
    slot_ids = jnp.arange(UNIQUE, dtype=jnp.int32)
    rate = 0.1 / math.sqrt(TOKENS)
    norm_ties = jnp.stack([tie_sources[param_index] for param_index in row_params])
    norm_grad = jnp.where(slot_ids[:, None, None] == norm_ties[None, :, None], sums[4][None], 0.0)
    head_grad = jnp.where((slot_ids == tie_sources[3])[:, None, None], sums[5][None], 0.0)
    hidden_grad = jnp.where((slot_ids == tie_sources[9])[:, None], sums[6][None], 0.0)
    new_norm_momentum = vector_decay * norm_momentum + norm_grad
    new_norm_vectors = norm_vectors - rate * new_norm_momentum
    new_head_bias_momentum = vector_decay * head_bias_momentum + head_grad
    new_head_bias = head_bias - rate * new_head_bias_momentum
    new_fc_bias_momentum = vector_decay * fc_bias_momentum + hidden_grad
    new_fc_bias = fc_bias - rate * new_fc_bias_momentum
    banks = ((attn_weight, attn_momentum, attn_average, sums[0], 2, 3 * D), (proj_weight, proj_momentum, proj_average, sums[1], 4, D), (fc_weight, fc_momentum, fc_average, sums[2], 8, FF), (out_weight, out_momentum, out_average, sums[3], 10, FF))
    results = []
    for kind_index, (weight_bank, momentum_bank, average_bank, grad_full, param_index, columns) in enumerate(banks):
        chosen = (slot_ids == tie_sources[param_index]).reshape((UNIQUE,) + (1,) * grad_full.ndim)
        renewed = matrix_decay * momentum_bank + jnp.where(chosen, grad_full[None], 0.0)
        updates = []
        for slot_index in range(UNIQUE):
            updates.append(join_halves(kind_index, newton(split_halves(kind_index, renewed[slot_index]))))
        factor = math.sqrt(columns / D)
        new_weight = weight_bank - factor * jnp.stack(updates).astype(jnp.float32)
        new_average = average_decay * average_bank + (1.0 - average_decay) * new_weight
        results.append((new_weight, renewed, new_average))
    return (block_output, input_grad, results[0][0], results[0][1], results[0][2], results[1][0], results[1][1], results[1][2], results[2][0], results[2][1], results[2][2], results[3][0], results[3][1], results[3][2], new_norm_vectors, new_norm_momentum, new_head_bias, new_head_bias_momentum, new_fc_bias, new_fc_bias_momentum)
```

```python
import functools
import math

import jax
import jax.numpy as jnp
from jax import lax
from jax.experimental import pallas as pl
from jax.experimental.pallas import tpu as pltpu
from jax.sharding import Mesh, PartitionSpec as P

D = 768
HEAD = 64
FF = 3072
LEN = 1024
NS_STEPS = 5
KINDS = 4


norm_epsilon = 1e-05
gelu_scale = 0.7978845608028654
coef_one = 3.4445
coef_three = -4.775
coef_five = 2.0315
row_params = (0, 1, 6, 7, 5, 11)
matrix_params = (2, 4, 8, 10)
PACKED = (2, 3, 1, 0)
update_factors = tuple(math.sqrt(columns / D) for columns in (3 * D, D, FF, FF))
vector_decay = 0.9
matrix_decay = 0.5
average_decay = 0.75
DP = ("plane", "lane")
f32 = jnp.float32
bf16 = jnp.bfloat16
PAIR = 128
TILE = 256
NT = (((1,), (1,)), ((), ()))
NN = (((1,), (0,)), ((), ()))


def layer_norm(values, gain_row, shift_row):
    centre = jnp.mean(values, axis=-1, keepdims=True)
    centred = values - centre
    spread = jnp.mean(centred * centred, axis=-1, keepdims=True)
    inverse = lax.rsqrt(spread + norm_epsilon)
    normed = centred * inverse
    return (normed * gain_row + shift_row, normed, inverse)


def norm_backward(grad_out, normed, inverse, gain_row):
    scaled = grad_out * gain_row
    row_inner = jnp.mean(scaled, axis=-1, keepdims=True)
    row_cross = jnp.mean(scaled * normed, axis=-1, keepdims=True)
    grad_in = inverse * (scaled - row_inner - normed * row_cross)
    return (grad_in, jnp.sum(grad_out * normed, axis=0), jnp.sum(grad_out, axis=0))


def product(left, right, dims=NN):
    return lax.dot_general(left, right, dims, preferred_element_type=f32)


def head_lanes(shape, axis, head):
    lane = lax.broadcasted_iota(jnp.int32, shape, axis)
    return (lane < HEAD) if head == 0 else (lane >= HEAD)


def causal(tile):
    key = lax.broadcasted_iota(jnp.int32, (tile, tile), 0)
    query = lax.broadcasted_iota(jnp.int32, (tile, tile), 1)
    return key <= query


def attend_kernel(query_ref, key_ref, value_ref, mixed_ref, total_ref):
    length = query_ref.shape[0]
    tile = min(TILE, length)
    value_t = value_ref[...].T
    keep = causal(tile)
    zero = jnp.zeros((), bf16)
    value_heads = [
        jnp.where(head_lanes(value_t.shape, 0, head), value_t, zero) for head in range(2)
    ]
    for first in range(0, length, tile):
        query = query_ref[first : first + tile, :] * jnp.asarray(HEAD**-0.5, bf16)
        mixed_t = jnp.zeros((PAIR, tile), f32)
        for head in range(2):
            query_head = jnp.where(head_lanes(query.shape, 1, head), query, zero)
            scores = []
            for at in range(0, first + tile, tile):
                score = product(key_ref[at : at + tile, :], query_head, NT)
                scores.append(jnp.where(keep, score, -1e30) if at == first else score)
            top = functools.reduce(
                jnp.maximum, [jnp.max(score, axis=0, keepdims=True) for score in scores]
            )
            weights = [jnp.exp(score - top) for score in scores]
            total = functools.reduce(
                jnp.add, [jnp.sum(weight, axis=0, keepdims=True) for weight in weights]
            )
            inverse = 1.0 / total
            for index, weight in enumerate(weights):
                at = index * tile
                mixed_t += product(
                    value_heads[head][:, at : at + tile], (weight * inverse).astype(bf16)
                )
            total_ref[0, head : head + 1, first : first + tile] = top + jnp.log(total)
        mixed_ref[first : first + tile, :] = mixed_t.T.astype(bf16)


def attend(triple, pair, pairs):
    length = triple.shape[0]

    def column(kind):
        return pl.BlockSpec((length, PAIR), lambda step: (0, kind * pairs + pair))

    return pl.pallas_call(
        attend_kernel,
        grid=(1,),
        in_specs=[column(0), column(1), column(2)],
        out_specs=[
            pl.BlockSpec((length, PAIR), lambda step: (0, 0)),
            pl.BlockSpec((1, 2, length), lambda step: (0, 0, 0)),
        ],
        out_shape=[
            jax.ShapeDtypeStruct((length, PAIR), bf16),
            jax.ShapeDtypeStruct((1, 2, length), f32),
        ],
        compiler_params=pltpu.CompilerParams(vmem_limit_bytes=40 << 20),
        cost_estimate=pl.CostEstimate(
            flops=8 * length * length * PAIR,
            bytes_accessed=8 * length * PAIR,
            transcendentals=length * length,
        ),
        name="attend",
    )(triple, triple, triple)


def attend_back_kernel(
    query_ref,
    key_ref,
    value_ref,
    grad0_ref,
    grad1_ref,
    input_ref,
    turned0_ref,
    turned1_ref,
    *refs,
):
    pairs = (len(refs) - 6) // 2
    out_ref, weight_ref, key_acc, value_acc, total_ref, mixed_ref = refs[2 * pairs :]
    for pair in range(pairs):

        @pl.when(pl.program_id(0) == pair)
        def _():
            total_ref[...] = refs[pair][...]
            mixed_ref[...] = refs[pairs + pair][...]

    length = query_ref.shape[0]
    tile = min(TILE, length)
    key_t = key_ref[...].T
    keep = causal(tile)
    zero = jnp.zeros((), bf16)
    scale = HEAD**-0.5
    key_heads = [jnp.where(head_lanes(key_t.shape, 0, head), key_t, zero) for head in range(2)]
    for first in range(0, length, tile):
        query = query_ref[first : first + tile, :] * jnp.asarray(scale, bf16)
        middle = grad0_ref.shape[0]
        if first < middle:
            grad = grad0_ref[first : first + tile, :]
        else:
            grad = grad1_ref[first - middle : first - middle + tile, :]
        query_grad_t = jnp.zeros((PAIR, tile), f32)
        key_parts = [None] * (first // tile + 1)
        value_parts = [None] * (first // tile + 1)
        for head in range(2):
            query_head = jnp.where(head_lanes(query.shape, 1, head), query, zero)
            grad_head = jnp.where(head_lanes(grad.shape, 1, head), grad, zero)
            total = total_ref[0, head : head + 1, first : first + tile]
            weights, weight_grads = [], []
            inner = jnp.zeros((1, tile), f32)
            for at in range(0, first + tile, tile):
                score = product(key_ref[at : at + tile, :], query_head, NT)
                weight = jnp.exp(score - total)
                if at == first:
                    weight = jnp.where(keep, weight, 0.0)
                weight_grad = product(value_ref[at : at + tile, :], grad_head, NT)
                inner += jnp.sum(weight * weight_grad, axis=0, keepdims=True)
                weights.append(weight)
                weight_grads.append(weight_grad)
            for index in range(first // tile + 1):
                at = index * tile
                score_grad = (weights[index] * (weight_grads[index] - inner)).astype(bf16)
                query_grad_t += product(key_heads[head][:, at : at + tile], score_grad)
                key_part = product(score_grad, query_head)
                value_part = product(weights[index].astype(bf16), grad_head)
                key_parts[index] = key_part if head == 0 else key_parts[index] + key_part
                value_parts[index] = value_part if head == 0 else value_parts[index] + value_part
        for index in range(first // tile + 1):
            at = index * tile
            if index == first // tile:
                key_acc[at : at + tile, :] = key_parts[index]
                value_acc[at : at + tile, :] = value_parts[index]
            else:
                key_acc[at : at + tile, :] += key_parts[index]
                value_acc[at : at + tile, :] += value_parts[index]
        out_ref[0, first : first + tile, :] = (query_grad_t * scale).T.astype(bf16)
    out_ref[1] = key_acc[...].astype(bf16)
    out_ref[2] = value_acc[...].astype(bf16)
    weight_ref[:, : 3 * PAIR] = product(
        input_ref[...], jnp.concatenate([out_ref[0], out_ref[1], out_ref[2]], axis=1)
    ).astype(bf16)
    weight_ref[:, 3 * PAIR :] = (
        product(turned0_ref[...], mixed_ref[:middle, :])
        + product(turned1_ref[...], mixed_ref[middle:, :])
    ).astype(bf16)


def attend_back(triple, mixed_grad, totals, turned_in, turned_mid, mixed, pairs):
    length = triple.shape[0]
    width = turned_in.shape[0]

    def column(kind):
        return pl.BlockSpec((length, PAIR), lambda pair: (0, kind * pairs + pair))

    half = pl.BlockSpec((length // 2, PAIR), lambda pair: (0, pair))
    turned = pl.BlockSpec((width, length // 2), lambda pair: (0, 0))
    return pl.pallas_call(
        attend_back_kernel,
        grid=(pairs,),
        in_specs=[
            column(0),
            column(1),
            column(2),
            half,
            half,
            pl.BlockSpec((width, length), lambda pair: (0, 0)),
            turned,
            turned,
        ]
        + [pl.BlockSpec((1, 2, length), lambda pair: (0, 0, 0))] * pairs
        + [pl.BlockSpec((length, PAIR), lambda pair: (0, 0))] * pairs,
        out_specs=[
            pl.BlockSpec((3, length, PAIR), lambda pair: (0, 0, pair)),
            pl.BlockSpec((width, 4 * PAIR), lambda pair: (0, pair)),
        ],
        out_shape=[
            jax.ShapeDtypeStruct((3, length, pairs * PAIR), bf16),
            jax.ShapeDtypeStruct((width, 4 * pairs * PAIR), bf16),
        ],
        scratch_shapes=[
            pltpu.VMEM((length, PAIR), f32),
            pltpu.VMEM((length, PAIR), f32),
            pltpu.VMEM((1, 2, length), f32),
            pltpu.VMEM((length, PAIR), bf16),
        ],
        compiler_params=pltpu.CompilerParams(vmem_limit_bytes=60 << 20),
        cost_estimate=pl.CostEstimate(
            flops=20 * pairs * length * length * PAIR,
            bytes_accessed=30 * pairs * length * PAIR,
            transcendentals=pairs * length * length,
        ),
        name="attend_back",
    )(triple, triple, triple, *mixed_grad, turned_in, *turned_mid, *totals, *mixed)


def gram_into(rows_ref, total_ref):
    size = rows_ref.shape[0]
    for at in range(0, size, TILE):
        total_ref[at:, at : at + TILE] = product(rows_ref[at:, :], rows_ref[at : at + TILE, :], NT)
    mirror(total_ref)


def mirror(total_ref):
    size = total_ref.shape[0]
    for at in range(0, size, TILE):
        for low in range(at + TILE, size, TILE):
            total_ref[at : at + TILE, low : low + TILE] = total_ref[
                low : low + TILE, at : at + TILE
            ].T


def identity(rows, columns):
    return lax.broadcasted_iota(jnp.int32, (rows, columns), 0) == lax.broadcasted_iota(
        jnp.int32, (rows, columns), 1
    )


def symmetric_product(left, right, total_ref):
    size = left.shape[0]
    for at in range(0, size, TILE):
        total_ref[at:, at : at + TILE] = product(left[at:], right[:, at : at + TILE])
    mirror(total_ref)
    return total_ref[...]


def with_linear(gram_low, square):
    mixing = coef_three * gram_low.astype(f32) + coef_five * square
    return jnp.where(identity(*mixing.shape), mixing + coef_one, mixing).astype(bf16)


def mixing_of(gram_low, total_ref):
    return with_linear(gram_low, symmetric_product(gram_low, gram_low, total_ref))


def grow(source_ref, made_ref, mixing, factor=None):
    width = source_ref.shape[1]
    chunk = 512 if width % 512 == 0 else width

    @pl.loop(0, width // chunk)
    def _(step):
        span = pl.ds(pl.multiple_of(step * chunk, chunk), chunk)
        grown = product(mixing, source_ref[:, span])
        made_ref[:, span] = (grown if factor is None else grown * factor).astype(bf16)


def next_gram(gram_low, mixing, total_ref):
    half = product(mixing, gram_low).astype(bf16)
    return symmetric_product(half, mixing, total_ref).astype(bf16)


def assemble(piece_refs, rows_ref):
    rows, span = piece_refs[0].shape[1:]
    for core in range(2):
        low, low_other, high, high_other = piece_refs[4 * core : 4 * core + 4]
        for row in range(2):
            at = (2 * core + row) * rows
            row_high = high if row == 0 else high_other
            rows_ref[at : at + rows, :span] = low[row]
            rows_ref[at : at + rows, span : 2 * span] = row_high[0]
            rows_ref[at : at + rows, 2 * span : 3 * span] = low_other[row]
            rows_ref[at : at + rows, 3 * span :] = row_high[1]


def first_rounds(rows_ref, total_ref):
    size = rows_ref.shape[0]
    gram_into(rows_ref, total_ref)
    diagonal = jnp.zeros((TILE, TILE), f32)
    on_diagonal = identity(TILE, TILE)
    for at in range(0, size, TILE):
        diagonal += jnp.where(on_diagonal, total_ref[at : at + TILE, at : at + TILE], 0.0)
    trace = jnp.sum(jnp.sum(diagonal, axis=0, keepdims=True), axis=1, keepdims=True)
    factor = lax.rsqrt(trace + 1e-07)
    gram_low = (total_ref[...] * factor * factor).astype(bf16)
    mixing = mixing_of(gram_low, total_ref)
    so_far = mixing
    for unused_round in range(2):
        gram_low = next_gram(gram_low, mixing, total_ref)
        mixing = mixing_of(gram_low, total_ref)
        so_far = symmetric_product(mixing, so_far, total_ref).astype(bf16)
    grow(rows_ref, rows_ref, so_far, factor)


def last_rounds(rows_ref, own_ref, total_ref):
    own_rows, own_columns = own_ref.shape
    gram_into(rows_ref, total_ref)
    gram_low = total_ref[...].astype(bf16)
    fourth = mixing_of(gram_low, total_ref)
    gram_low = next_gram(gram_low, fourth, total_ref)
    top = gram_low[:own_rows]
    fifth = with_linear(top, product(top, gram_low))
    both = product(fifth, fourth).astype(bf16)
    own_ref[...] = product(both, rows_ref[:, :own_columns]).astype(bf16)


def first_kernel(*refs):
    *piece_refs, rows_ref, total_ref = refs
    assemble(piece_refs, rows_ref)
    first_rounds(rows_ref, total_ref)


def last_kernel(rows_ref, own_ref, total_ref):
    last_rounds(rows_ref, own_ref, total_ref)


def all_kernel(*refs):
    *piece_refs, own_ref, rows_ref, total_ref = refs
    assemble(piece_refs, rows_ref)
    first_rounds(rows_ref, total_ref)
    last_rounds(rows_ref, own_ref, total_ref)


def newton_call(kernel, operands, out_shape, size, width, work, scratch=()):
    return pl.pallas_call(
        kernel,
        in_specs=[pl.BlockSpec(memory_space=pltpu.VMEM)] * len(operands),
        out_specs=pl.BlockSpec(memory_space=pltpu.VMEM),
        out_shape=jax.ShapeDtypeStruct(out_shape, bf16),
        scratch_shapes=[*scratch, pltpu.VMEM((size, size), f32)],
        compiler_params=pltpu.CompilerParams(vmem_limit_bytes=60 << 20),
        cost_estimate=pl.CostEstimate(
            flops=work * size * size * width, bytes_accessed=4 * size * width, transcendentals=0
        ),
        name="newton",
    )(*operands)


def swap_tensor(block):
    return lax.ppermute(block, "tensor", [(0, 1), (1, 0)])


def swap_lane(block, bit):
    count = lax.axis_size("lane")
    return lax.ppermute(block, "lane", [(lane, lane ^ (1 << bit)) for lane in range(count)])


def rows_swapped(block, bit):
    return jnp.concatenate([block, swap_lane(block, bit)], axis=0)


def gate(value, *others):
    count = len(others)

    def kernel(*refs):
        del refs

    anywhere = pl.BlockSpec(memory_space=pl.ANY)
    return pl.pallas_call(
        kernel,
        in_specs=[anywhere] * (count + 1),
        out_specs=anywhere,
        out_shape=jax.ShapeDtypeStruct(value.shape, value.dtype),
        input_output_aliases={0: 0},
        cost_estimate=pl.CostEstimate(flops=0, bytes_accessed=0, transcendentals=0),
        name="gate",
    )(value, *others)


def normed_rows(values):
    centred = values - jnp.mean(values, axis=-1, keepdims=True)
    inverse = lax.rsqrt(jnp.mean(centred * centred, axis=-1, keepdims=True) + norm_epsilon)
    return centred * inverse, inverse


def mlp_kernel(
    side_ref,
    token_ref,
    own0_ref,
    own1_ref,
    own2_ref,
    other0_ref,
    other1_ref,
    other2_ref,
    own_proj_ref,
    other_proj_ref,
    fc_ref,
    out_ref,
    norm_ref,
    bias_ref,
    grad_ref,
    mid_ref,
    in_ref,
    act_ref,
    hidden_grad_ref,
    back_ref,
    part_ref,
    sum_ref,
    back_acc,
    part_acc,
):
    step = pl.program_id(0)

    @pl.when(step == 0)
    def _():
        is_low = side_ref[0] == 0
        own, other = own_proj_ref[...], other_proj_ref[...]
        proj = jnp.concatenate(
            [jnp.where(is_low, own, other), jnp.where(is_low, other, own)], axis=1
        )
        own = jnp.concatenate([own0_ref[...], own1_ref[...], own2_ref[...]], axis=1)
        other = jnp.concatenate([other0_ref[...], other1_ref[...], other2_ref[...]], axis=1)
        mixed = jnp.concatenate(
            [jnp.where(is_low, own, other), jnp.where(is_low, other, own)], axis=1
        )
        mid = token_ref[...].astype(f32) + (product(mixed, proj, NT) + norm_ref[4:5, :])
        mid_ref[...] = mid
        normed, inverse = normed_rows(mid)
        in_ref[...] = (normed * norm_ref[2:3, :] + norm_ref[3:4, :]).astype(bf16)

    fc_part, out_part = fc_ref[...], out_ref[...]
    values = product(in_ref[...], fc_part) + bias_ref[...]
    square = values * values
    curve = jnp.tanh(gelu_scale * (values + 0.044715 * values * square))
    gate_up = 0.5 * (1.0 + curve)
    act = (values * gate_up).astype(bf16)
    act_ref[...] = act
    slope = gate_up + (0.5 * gelu_scale) * values * (1.0 - curve * curve) * (
        1.0 + (3.0 * 0.044715) * square
    )
    hidden_grad = (product(grad_ref[...], out_part) * slope).astype(bf16)
    hidden_grad_ref[...] = hidden_grad
    sum_ref[...] = jnp.sum(hidden_grad.astype(f32), axis=0, keepdims=True)
    back = product(hidden_grad, fc_part, NT)
    part = product(act, out_part, NT)

    @pl.when(step == 0)
    def _():
        back_acc[...] = back
        part_acc[...] = part

    @pl.when(step > 0)
    def _():
        back_acc[...] += back
        part_acc[...] += part

    @pl.when(step == pl.num_programs(0) - 1)
    def _():
        back_ref[...] = back_acc[...].astype(bf16)
        part_ref[...] = part_acc[...].astype(bf16)


def mlp(side, tokens, own, other, full, norm_rows, hidden_bias, grads, chunk, chunks):
    rows, width = tokens.shape
    hidden = hidden_bias.shape[1]
    half = PAIR * len(own)
    part_rows = rows // chunks
    steps = 3
    span = hidden // steps

    def tall(columns):
        return pl.BlockSpec((part_rows, columns), lambda step: (chunk, 0))

    def fixed(shape, column=0):
        return pl.BlockSpec(shape, lambda step: (0, column))

    def moving(size, first=0):
        return pl.BlockSpec((size, span), lambda step: (0, first + step))

    return pl.pallas_call(
        mlp_kernel,
        grid=(steps,),
        in_specs=[pl.BlockSpec(memory_space=pltpu.SMEM), tall(width)]
        + [tall(PAIR)] * 6
        + [
            fixed((width, half), 2 * hidden // half),
            fixed((width, half), full.shape[1] // half - 1),
            moving(width),
            moving(width, steps),
            fixed((6, width)),
            moving(1),
            tall(width),
        ],
        out_specs=[
            fixed((part_rows, width)),
            fixed((part_rows, width)),
            moving(part_rows),
            moving(part_rows),
            fixed((part_rows, width)),
            fixed((part_rows, width)),
            moving(1),
        ],
        out_shape=[
            jax.ShapeDtypeStruct((part_rows, width), f32),
            jax.ShapeDtypeStruct((part_rows, width), bf16),
            jax.ShapeDtypeStruct((part_rows, hidden), bf16),
            jax.ShapeDtypeStruct((part_rows, hidden), bf16),
            jax.ShapeDtypeStruct((part_rows, width), bf16),
            jax.ShapeDtypeStruct((part_rows, width), bf16),
            jax.ShapeDtypeStruct((1, hidden), f32),
        ],
        scratch_shapes=[pltpu.VMEM((part_rows, width), f32), pltpu.VMEM((part_rows, width), f32)],
        compiler_params=pltpu.CompilerParams(vmem_limit_bytes=60 << 20),
        cost_estimate=pl.CostEstimate(
            flops=10 * part_rows * width * hidden,
            bytes_accessed=4 * width * hidden + 20 * part_rows * width,
            transcendentals=part_rows * hidden,
        ),
        name="mlp",
    )(side, tokens, *own, *other, full, full, full, full, norm_rows, hidden_bias, grads)


def weight_kernel(in0_ref, in1_ref, grad_ref, hidden0_ref, hidden1_ref, act0_ref, act1_ref, made_ref, turned_ref):
    step = pl.program_id(0)
    half = pl.num_programs(0) // 2
    rows = in0_ref.shape[0]

    @pl.when(step == 0)
    def _():
        turned_ref[:, :rows] = in0_ref[...].T
        turned_ref[:, rows:] = in1_ref[...].T

    @pl.when(step == half)
    def _():
        turned_ref[...] = grad_ref[...].T

    @pl.when(step < half)
    def _():
        made_ref[...] = product(
            turned_ref[...], jnp.concatenate([hidden0_ref[...], hidden1_ref[...]], axis=0)
        ).astype(bf16)

    @pl.when(step >= half)
    def _():
        made_ref[...] = product(
            turned_ref[...], jnp.concatenate([act0_ref[...], act1_ref[...]], axis=0)
        ).astype(bf16)


def weight_grads(mlp_in, grads, hidden_grad, act):
    rows, width = mlp_in[0].shape
    hidden = act[0].shape[1]
    span = hidden // 3
    whole = pl.BlockSpec((rows, width), lambda step: (0, 0))
    early = pl.BlockSpec((rows, span), lambda step: (0, jnp.minimum(step, 2)))
    late = pl.BlockSpec((rows, span), lambda step: (0, jnp.maximum(step - 3, 0)))
    return pl.pallas_call(
        weight_kernel,
        grid=(6,),
        in_specs=[whole, whole, pl.BlockSpec((2 * rows, width), lambda step: (0, 0))]
        + [early] * 2
        + [late] * 2,
        out_specs=pl.BlockSpec((width, span), lambda step: (0, step)),
        out_shape=jax.ShapeDtypeStruct((width, 2 * hidden), bf16),
        scratch_shapes=[pltpu.VMEM((width, 2 * rows), bf16)],
        compiler_params=pltpu.CompilerParams(vmem_limit_bytes=60 << 20),
        cost_estimate=pl.CostEstimate(
            flops=8 * rows * width * hidden,
            bytes_accessed=8 * rows * hidden + 4 * width * hidden,
            transcendentals=0,
        ),
        name="weight_grads",
    )(*mlp_in, grads, *hidden_grad, *act)


def middle_kernel(own_ref, other_ref, mid_ref, grad_ref, norm_ref, proj_ref, e1_ref, turned_ref, mixed_ref, sum_ref):
    @pl.when(pl.program_id(0) == 0)
    def _():
        sum_ref[...] = jnp.zeros_like(sum_ref)

    back = own_ref[...].astype(f32) + other_ref[...].astype(f32)
    grad = grad_ref[...].astype(f32)
    normed, inverse = normed_rows(mid_ref[...])
    scaled = back * norm_ref[2:3, :]
    inner = jnp.mean(scaled, axis=-1, keepdims=True)
    cross = jnp.mean(scaled * normed, axis=-1, keepdims=True)
    e1 = grad + inverse * (scaled - inner - normed * cross)
    e1_ref[...] = e1
    low = e1.astype(bf16)
    turned_ref[...] = low.T
    mixed_ref[...] = product(low, proj_ref[...]).astype(bf16)
    for row, term in enumerate((back * normed, back, e1, grad)):
        sum_ref[row : row + 1, :] += jnp.sum(term, axis=0, keepdims=True)


def middle(own, other, mid, grads, norm_rows, full, half, chunk):
    rows, width = own.shape
    tile = min(TILE, rows)
    steps = rows // tile
    column = full.shape[1] // half - 2
    plain = pl.BlockSpec((tile, width), lambda step: (step, 0))
    return pl.pallas_call(
        middle_kernel,
        grid=(steps,),
        in_specs=[
            plain,
            plain,
            plain,
            pl.BlockSpec((tile, width), lambda step: (chunk * steps + step, 0)),
            pl.BlockSpec((6, width), lambda step: (0, 0)),
            pl.BlockSpec((width, half), lambda step: (0, column)),
        ],
        out_specs=[
            plain,
            pl.BlockSpec((width, tile), lambda step: (0, step)),
            pl.BlockSpec((tile, half), lambda step: (step, 0)),
            pl.BlockSpec((4, width), lambda step: (0, 0)),
        ],
        out_shape=[
            jax.ShapeDtypeStruct((rows, width), f32),
            jax.ShapeDtypeStruct((width, rows), bf16),
            jax.ShapeDtypeStruct((rows, half), bf16),
            jax.ShapeDtypeStruct((4, width), f32),
        ],
        compiler_params=pltpu.CompilerParams(vmem_limit_bytes=60 << 20),
        cost_estimate=pl.CostEstimate(
            flops=2 * rows * width * half, bytes_accessed=18 * rows * width, transcendentals=0
        ),
        name="middle",
    )(own, other, mid, grads, norm_rows, full)


def bank_rows(kind, bank):
    if kind == 0:
        return bank.transpose(0, 2, 1, 3)
    return bank if kind == 2 else jnp.swapaxes(bank, 1, 2)


def rows_of(kind, ref, slot=0):
    if kind == 0:
        return jnp.concatenate([ref[slot, part] for part in range(3)], axis=1)
    return ref[slot]


def pack_kernel(tie_ref, *refs, scale, padded, kinds):
    del tie_ref
    *bank_refs, made_ref = refs
    at = 0
    for kind, ref in zip(kinds, bank_refs):
        rows = rows_of(kind, ref) * scale
        width = rows.shape[1]
        if padded:
            made_ref[kind] = jnp.zeros(made_ref.shape[1:], made_ref.dtype)
            made_ref[kind, :, :width] = rows.astype(made_ref.dtype)
        else:
            made_ref[:, at : at + width] = rows.astype(made_ref.dtype)
        at += width


def pack(tie_sources, banks, other, scale, kind_of, padded=0, kinds=PACKED):
    def spec(kind):
        param = matrix_params[kind]

        def index(step, tie_ref):
            slot = tie_ref[param]
            return (1 - slot if other else slot,) + (0,) * (banks[kind].ndim - 1)

        return pl.BlockSpec((1,) + banks[kind].shape[1:], index)

    shard_rows = banks[0].shape[2]
    width = sum(banks[kind][0].size // shard_rows for kind in kinds)
    shape = (KINDS, shard_rows, padded) if padded else (shard_rows, width)
    return pl.pallas_call(
        functools.partial(pack_kernel, scale=scale, padded=padded, kinds=kinds),
        grid_spec=pltpu.PrefetchScalarGridSpec(
            num_scalar_prefetch=1,
            grid=(1,),
            in_specs=[spec(kind) for kind in kinds],
            out_specs=pl.BlockSpec(shape, lambda step, tie_ref: (0,) * len(shape)),
        ),
        out_shape=jax.ShapeDtypeStruct(shape, kind_of),
        compiler_params=pltpu.CompilerParams(vmem_limit_bytes=60 << 20),
        cost_estimate=pl.CostEstimate(
            flops=0, bytes_accessed=16 * shard_rows * width, transcendentals=0
        ),
        name="pack",
    )(tie_sources, *[banks[kind] for kind in kinds])


def collect_kernel(first_ref, low_ref, high_ref, triple_ref, hidden0_ref, hidden1_ref, made_ref):
    width = made_ref.shape[1]
    half = triple_ref.shape[2]
    made_ref[0:2, :] = first_ref[...]
    made_ref[2:6, :] = low_ref[...] + high_ref[...]
    made_ref[6:7, :half] = jnp.sum(triple_ref[0].astype(f32), axis=0, keepdims=True)
    made_ref[6:7, half:] = jnp.sum(triple_ref[2].astype(f32), axis=0, keepdims=True)
    for row in range(2):
        span = slice(row * width, (row + 1) * width)
        made_ref[7 + row : 8 + row, :] = hidden0_ref[:, span] + hidden1_ref[:, span]


def collect(*terms):
    width = terms[0].shape[1]
    return pl.pallas_call(
        collect_kernel,
        in_specs=[pl.BlockSpec(memory_space=pltpu.VMEM)] * len(terms),
        out_specs=pl.BlockSpec(memory_space=pltpu.VMEM),
        out_shape=jax.ShapeDtypeStruct((9, width), f32),
        compiler_params=pltpu.CompilerParams(vmem_limit_bytes=60 << 20),
        cost_estimate=pl.CostEstimate(flops=0, bytes_accessed=2 * terms[3].size, transcendentals=0),
        name="collect",
    )(*terms)


def momentum_kernel(reduced_ref, second_ref, decayed_ref, rows_ref, sent_ref, *, half, pairs):
    hidden = sent_ref.shape[2]
    reduced = reduced_ref[0].astype(f32)
    for plane in range(1, KINDS):
        reduced += reduced_ref[plane].astype(f32)
    ordered = [
        reduced[:, (4 * pair + part) * PAIR : (4 * pair + part + 1) * PAIR]
        for part in (3, 0, 1, 2)
        for pair in range(pairs)
    ]
    first = jnp.concatenate(ordered, axis=1)
    rows_ref[:, : 2 * hidden] = decayed_ref[:, : 2 * hidden] + second_ref[...].astype(f32)
    rows_ref[:, 2 * hidden :] = decayed_ref[:, 2 * hidden :] + first
    sent_ref[...] = jnp.zeros_like(sent_ref)
    sent_ref[2] = rows_ref[:, :hidden].astype(bf16)
    sent_ref[3] = rows_ref[:, hidden : 2 * hidden].astype(bf16)
    sent_ref[1, :, :half] = rows_ref[:, 2 * hidden : 2 * hidden + half].astype(bf16)
    sent_ref[0, :, : 3 * half] = rows_ref[:, 2 * hidden + half :].astype(bf16)


def new_momentum(reduced, second, decayed, half):
    shard_rows, width = decayed.shape
    hidden = second.shape[1] // 2
    return pl.pallas_call(
        functools.partial(momentum_kernel, half=half, pairs=half // PAIR),
        in_specs=[pl.BlockSpec(memory_space=pltpu.VMEM)] * 3,
        out_specs=[pl.BlockSpec(memory_space=pltpu.VMEM)] * 2,
        out_shape=[
            jax.ShapeDtypeStruct((shard_rows, width), f32),
            jax.ShapeDtypeStruct((KINDS, shard_rows, hidden), bf16),
        ],
        compiler_params=pltpu.CompilerParams(vmem_limit_bytes=60 << 20),
        cost_estimate=pl.CostEstimate(
            flops=0, bytes_accessed=16 * shard_rows * width, transcendentals=0
        ),
        name="new_momentum",
    )(reduced, second, decayed)


def input_grad_kernel(triple_ref, weight_ref, made_ref):
    grads = jnp.concatenate([triple_ref[0], triple_ref[1], triple_ref[2]], axis=1)
    made_ref[...] = product(grads, weight_ref[...], NT).astype(bf16)


def input_grads(triple_grad, full):
    kinds, rows, half = triple_grad.shape
    width = full.shape[0]
    tile = min(2 * TILE, rows)
    return pl.pallas_call(
        input_grad_kernel,
        grid=(rows // tile,),
        in_specs=[
            pl.BlockSpec((kinds, tile, half), lambda step: (0, step, 0)),
            pl.BlockSpec((width, kinds * half), lambda step: (0, 0)),
        ],
        out_specs=pl.BlockSpec((tile, width), lambda step: (step, 0)),
        out_shape=jax.ShapeDtypeStruct((rows, width), bf16),
        compiler_params=pltpu.CompilerParams(vmem_limit_bytes=60 << 20),
        cost_estimate=pl.CostEstimate(
            flops=2 * rows * width * kinds * half, bytes_accessed=8 * rows * width, transcendentals=0
        ),
        name="input_grads",
    )(triple_grad, full)


def finish_kernel(
    token_ref,
    first_ref,
    other_first_ref,
    mid_ref,
    part_ref,
    other_part_ref,
    e1_ref,
    norm_ref,
    *refs,
):
    out_ref, grad_ref, sum_ref = refs[-3:]

    @pl.when(pl.program_id(0) == 0)
    def _():
        sum_ref[...] = jnp.zeros_like(sum_ref)

    out_ref[...] = (
        mid_ref[...]
        + (part_ref[...].astype(f32) + other_part_ref[...].astype(f32) + norm_ref[5:6, :])
    ).astype(bf16)
    back = first_ref[...].astype(f32) + other_first_ref[...].astype(f32)
    normed, inverse = normed_rows(token_ref[...].astype(f32))
    scaled = back * norm_ref[0:1, :]
    inner = jnp.mean(scaled, axis=-1, keepdims=True)
    cross = jnp.mean(scaled * normed, axis=-1, keepdims=True)
    grad_ref[...] = (e1_ref[...] + inverse * (scaled - inner - normed * cross)).astype(bf16)
    for row, term in enumerate((back * normed, back)):
        sum_ref[row : row + 1, :] += jnp.sum(term, axis=0, keepdims=True)


def finish(tokens, first, other_first, mids, parts, other_parts, e1, norm_rows):
    rows, width = tokens.shape
    half = rows // 2
    tile = min(TILE, half)
    steps = half // tile

    def whole(chunk):
        return pl.BlockSpec((tile, width), lambda step: (chunk * steps + step, 0))

    plain = pl.BlockSpec((tile, width), lambda step: (step, 0))
    made, sums = [], []
    for chunk in range(2):
        *made, total = pl.pallas_call(
            finish_kernel,
            grid=(steps,),
            in_specs=[whole(chunk)] * 3
            + [plain] * 4
            + [pl.BlockSpec((6, width), lambda step: (0, 0))]
            + [pl.BlockSpec(memory_space=pl.ANY)] * len(made),
            out_specs=[
                whole(chunk),
                whole(chunk),
                pl.BlockSpec((2, width), lambda step: (0, 0)),
            ],
            out_shape=[
                jax.ShapeDtypeStruct((rows, width), bf16),
                jax.ShapeDtypeStruct((rows, width), bf16),
                jax.ShapeDtypeStruct((2, width), f32),
            ],
            input_output_aliases={8: 0, 9: 1} if made else {},
            compiler_params=pltpu.CompilerParams(vmem_limit_bytes=60 << 20),
            cost_estimate=pl.CostEstimate(
                flops=40 * half * width, bytes_accessed=22 * half * width, transcendentals=0
            ),
            name="finish",
        )(
            tokens,
            first,
            other_first,
            mids[chunk],
            parts[chunk],
            other_parts[chunk],
            e1[chunk],
            norm_rows,
            *made,
        )
        sums.append(total)
    return (*made, sums[0] + sums[1])


def put_rows(kind, ref, slot, rows):
    if kind == 0:
        half = ref.shape[3]
        for part in range(3):
            ref[slot, part] = rows[:, part * half : (part + 1) * half]
    else:
        ref[slot] = rows


def momentum_out_kernel(tie_ref, rows_ref, *refs):
    at = 0
    for kind, bank_ref, made_ref in zip(PACKED, refs[:KINDS], refs[KINDS:]):
        width = bank_ref[0].size // rows_ref.shape[0]
        renewed = rows_ref[:, at : at + width]
        at += width
        for slot in range(bank_ref.shape[0]):
            chosen = tie_ref[matrix_params[kind]] == slot

            @pl.when(chosen)
            def _():
                put_rows(kind, made_ref, slot, renewed)

            @pl.when(jnp.logical_not(chosen))
            def _():
                made_ref[slot] = matrix_decay * bank_ref[slot]


def weight_out_kernel(tie_ref, chosen_ref, kept_ref, *refs):
    weight_refs, average_refs = refs[:KINDS], refs[KINDS : 2 * KINDS]
    new_refs, mean_refs = refs[2 * KINDS : 3 * KINDS], refs[3 * KINDS :]
    for kind in range(KINDS):
        width = weight_refs[kind][0].size // chosen_ref.shape[1]
        for slot in range(weight_refs[kind].shape[0]):
            chosen = tie_ref[matrix_params[kind]] == slot
            rows = jnp.where(chosen, chosen_ref[kind, :, :width], kept_ref[kind, :, :width])
            step = (-update_factors[kind]) * rows.astype(f32)
            new = rows_of(kind, weight_refs[kind], slot) + step
            put_rows(kind, new_refs[kind], slot, new)
            mean = average_decay * rows_of(kind, average_refs[kind], slot)
            put_rows(kind, mean_refs[kind], slot, mean + (1.0 - average_decay) * new)


def out_call(kernel, tie_sources, operands, banks, name):
    inside = pl.BlockSpec(memory_space=pltpu.VMEM)
    size = sum(bank.size for bank in banks)
    return pl.pallas_call(
        kernel,
        in_specs=[pl.BlockSpec(memory_space=pltpu.SMEM)] + [inside] * len(operands),
        out_specs=[inside] * len(banks),
        out_shape=[jax.ShapeDtypeStruct(bank.shape, f32) for bank in banks],
        compiler_params=pltpu.CompilerParams(vmem_limit_bytes=60 << 20),
        cost_estimate=pl.CostEstimate(flops=0, bytes_accessed=12 * size, transcendentals=0),
        name=name,
    )(tie_sources, *operands)


def arrange_kernel(*refs, count):
    *pieces, out_ref = refs
    plane, lane = lax.axis_index("plane"), lax.axis_index("lane")
    for flip, piece in enumerate(pieces):
        for shift in range(KINDS):
            out_ref[lax.rem(plane + KINDS - shift, KINDS) * count + (lane ^ flip)] = piece[shift]


def dp_gather(rows, *sooner):
    count = lax.axis_size("lane")
    size, width = rows.shape
    if size % 16:
        made = lax.all_gather(rows, DP, axis=0, tiled=True)
        return made, made
    planes = jnp.stack(
            [rows]
            + [
                lax.ppermute(
                    rows, "plane", [(plane, (plane + shift) % KINDS) for plane in range(KINDS)]
                )
                for shift in range(1, KINDS)
            ]
    )
    pieces = [planes]
    order = [0]
    for bit in reversed(range(count.bit_length() - 1)):
        if bit == 0:
            pieces[-1] = gate(pieces[-1], *sooner)
        pieces += [swap_lane(piece, bit) for piece in pieces]
        order += [flip | (1 << bit) for flip in order]
    pieces = [piece for unused_flip, piece in sorted(zip(order, pieces), key=lambda pair: pair[0])]
    made = pl.pallas_call(
        functools.partial(arrange_kernel, count=count),
        in_specs=[pl.BlockSpec(memory_space=pltpu.VMEM)] * count,
        out_specs=pl.BlockSpec(memory_space=pltpu.VMEM),
        out_shape=jax.ShapeDtypeStruct((KINDS * count, size, width), bf16),
        compiler_params=pltpu.CompilerParams(vmem_limit_bytes=60 << 20),
        cost_estimate=pl.CostEstimate(
            flops=0, bytes_accessed=4 * KINDS * count * size * width, transcendentals=0
        ),
        name="arrange",
    )(*pieces)
    return made.reshape(KINDS * count * size, width), planes


def axis_sum(terms, axis):
    count = lax.axis_size(axis)

    def swapped(flip):
        return lax.ppermute(terms, axis, [(place, place ^ flip) for place in range(count)])

    for bit in range(2, count.bit_length() - 1):
        terms = terms + swapped(1 << bit)
    return (terms + swapped(1)) + (swapped(2) + swapped(3))


def lane_reduce(part, shard_rows):
    width = part.shape[1]
    lane = lax.axis_index("lane")
    lane_bits = lax.axis_size("lane").bit_length() - 1
    stages = []
    for bit in range(lane_bits):
        view = part.reshape(-1, 2, shard_rows, width)
        own_bit = (lane >> bit) & 1
        kept = lax.dynamic_index_in_dim(view, own_bit, 1, keepdims=False)
        sent = lax.dynamic_index_in_dim(view, 1 - own_bit, 1, keepdims=False)
        part = (kept.astype(f32) + swap_lane(sent, bit).astype(f32)).astype(bf16)
        stages.append(part)
    return part.reshape(KINDS, shard_rows, width), stages


def plane_rows(outgoing):
    arrived = lax.all_to_all(outgoing, "plane", split_axis=0, concat_axis=0, tiled=True)
    return arrived.reshape(-1, outgoing.shape[2])


def plane_gather(block, waits=(), last=()):
    lane_bits = lax.axis_size("lane").bit_length() - 1
    if waits and waits[0]:
        block = gate(block, *waits[0])
    for bit in range(2, lane_bits):
        block = rows_swapped(block, bit)
    middle = block.shape[1] // 2
    low, high = block[:, :middle], block[:, middle:]
    low_other, high_other = swap_lane(low, 1), swap_tensor(high)
    if waits:
        low, high = gate(low, *waits[1]), gate(high, *waits[1])
    low = jnp.stack([low, low_other])
    high = jnp.stack([high, high_other])
    mine = [low, swap_tensor(low), high, swap_lane(high, 1)]
    if last:
        mine[3] = gate(mine[3], *last)
    return mine + [swap_lane(piece, 0) for piece in mine]


def returned(own, shard_rows):
    own = own[: KINDS * shard_rows].reshape(KINDS, shard_rows, -1)
    return lax.all_to_all(own, "plane", split_axis=0, concat_axis=0, tiled=True)


def per_device(
    tokens,
    cotangent,
    tie_sources,
    attn_weight,
    attn_momentum,
    attn_average,
    proj_weight,
    proj_momentum,
    proj_average,
    fc_weight,
    fc_momentum,
    fc_average,
    out_weight,
    out_momentum,
    out_average,
    norm_vectors,
    norm_momentum,
    head_bias,
    head_bias_momentum,
    fc_bias,
    fc_bias_momentum,
):
    row_count, model_width = tokens.shape
    dp_count = lax.axis_size("plane") * lax.axis_size("lane")
    shard_rows = model_width // dp_count
    half_width = proj_weight.shape[1]
    hidden_half = fc_weight.shape[2]
    widths = (3 * half_width, half_width, hidden_half, hidden_half)
    slot_count = attn_weight.shape[0]

    def choose_slot(bank, param_index):
        return lax.dynamic_index_in_dim(bank, tie_sources[param_index], 0, keepdims=False)

    weight_banks, momentum_banks, average_banks = (
        [bank_rows(kind, bank) for kind, bank in enumerate(banks)]
        for banks in (
            (attn_weight, proj_weight, fc_weight, out_weight),
            (attn_momentum, proj_momentum, fc_momentum, out_momentum),
            (attn_average, proj_average, fc_average, out_average),
        )
    )
    norm_rows = jnp.stack(
        [
            norm_vectors[tie_sources[param_index], row_index]
            for row_index, param_index in enumerate(row_params)
        ]
    )

    attn_rows = pack(tie_sources, weight_banks, False, 1.0, bf16, kinds=PACKED[3:])
    low_rows = pack(tie_sources, weight_banks, False, 1.0, bf16, kinds=PACKED[:3])
    inputs = tokens.astype(f32)
    attn_normed, unused_unit, unused_inverse = layer_norm(inputs, norm_rows[0], norm_rows[1])
    attn_in = attn_normed.astype(bf16)
    turned_in = attn_in.T
    decayed_rows = pack(tie_sources, momentum_banks, False, matrix_decay, f32)
    kept_out = pack(tie_sources, momentum_banks, True, matrix_decay, bf16, hidden_half)
    attn_full, attn_planes = dp_gather(attn_rows, turned_in, decayed_rows, kept_out)
    other_proj_rows = swap_tensor(low_rows[:, 2 * hidden_half :])
    full = lax.all_gather(
        gate(jnp.concatenate([low_rows, other_proj_rows], axis=1), attn_planes),
        DP,
        axis=0,
        tiled=True,
    )
    pairs = half_width // PAIR

    query_bias = choose_slot(head_bias, 3)
    hidden_bias = choose_slot(fc_bias, 9)
    projected = jnp.dot(attn_in, attn_full, preferred_element_type=f32)
    bias_row = jnp.concatenate([query_bias[0], jnp.zeros_like(query_bias[0]), query_bias[1]])
    triple = (projected + bias_row[None]).astype(bf16)
    own_mixed, other_mixed, log_totals = [], [], []
    for pair in range(pairs):
        mixed, totals = attend(triple, pair, pairs)
        own_mixed.append(mixed)
        other_mixed.append(swap_tensor(mixed))
        log_totals.append(totals)

    kept_rows = plane_rows(gate(kept_out, full))
    side = lax.axis_index("tensor").astype(jnp.int32).reshape(1)
    mids, mlp_in, act, hidden_grad, backs, other_backs, parts, hidden_terms = zip(
        *[
            (made[0], made[1], made[2], made[3], made[4], swap_tensor(made[4]), made[5], made[6])
            for made in (
                mlp(
                    side,
                    tokens,
                    own_mixed,
                    other_mixed,
                    full,
                    norm_rows,
                    hidden_bias[None],
                    cotangent,
                    chunk,
                    2,
                )
                for chunk in range(2)
            )
        ]
    )
    second_part = weight_grads(
        (gate(mlp_in[0], other_backs[0], kept_rows), mlp_in[1]), cotangent, hidden_grad, act
    )
    second_shard = lax.psum_scatter(second_part, DP, scatter_dimension=0, tiled=True)
    e1, turned_mid, mixed_grad, middle_terms = zip(
        *[
            middle(
                backs[chunk],
                other_backs[chunk],
                mids[chunk],
                cotangent,
                norm_rows,
                full,
                half_width,
                chunk,
            )
            for chunk in range(2)
        ]
    )
    other_parts = [swap_tensor(gate(part, *mixed_grad)) for part in parts]
    kept_pieces = plane_gather(kept_rows, [other_backs[1:], mixed_grad])
    triple_grad, attn_grad = attend_back(
        triple,
        (mixed_grad[0], gate(mixed_grad[1], second_part)),
        log_totals,
        turned_in,
        turned_mid,
        own_mixed,
        pairs,
    )
    part, stages = lane_reduce(
        gate(attn_grad, kept_pieces[1], kept_pieces[3], other_parts[0]), shard_rows
    )
    first_part = input_grads(triple_grad, attn_full)
    other_first = swap_tensor(first_part)
    whole_shape = (model_width, 2 * hidden_half)
    own_shape = (-(-KINDS * shard_rows // 16) * 16, hidden_half)
    kept_whole = newton_call(
        first_kernel,
        [gate(kept_pieces[0], stages[0])] + kept_pieces[1:],
        whole_shape,
        *whole_shape,
        8,
    )
    first_shard = lax.all_to_all(
        gate(part, kept_whole, *other_parts), "plane", split_axis=0, concat_axis=0, tiled=True
    )
    kept_own = newton_call(
        last_kernel, [gate(kept_whole, stages[-1])], own_shape, *whole_shape, 4
    )
    renewed_rows, outgoing = new_momentum(
        gate(first_shard, other_first, kept_own), second_shard, decayed_rows, half_width
    )
    chosen_rows = plane_rows(outgoing)
    block_output, input_grad, norm_one_terms = finish(
        tokens,
        first_part,
        other_first,
        mids,
        parts,
        other_parts,
        e1,
        gate(norm_rows, renewed_rows),
    )
    collected = collect(norm_one_terms, *middle_terms, triple_grad, *hidden_terms)
    lane_terms = axis_sum(collected, "lane")
    terms = axis_sum(lane_terms, "plane")
    ordered = [momentum_banks[kind] for kind in PACKED]
    new_moments = out_call(
        momentum_out_kernel,
        tie_sources,
        [gate(renewed_rows, lane_terms)] + ordered,
        ordered,
        "momentum_out",
    )
    chosen_pieces = plane_gather(
        gate(chosen_rows, collected), [(), (lane_terms,)], [terms, *new_moments]
    )
    new_moments = [new_moments[PACKED.index(kind)] for kind in range(KINDS)]
    kept_updates = returned(gate(kept_own, chosen_pieces[0]), shard_rows)
    norm_grad = terms[:6]
    bias_grad = terms[6].reshape(2, half_width)
    fc_bias_grad = terms[7:].reshape(hidden_half)

    slot_ids = jnp.arange(slot_count, dtype=jnp.int32)
    rate = 0.1 / math.sqrt(row_count * dp_count)
    norm_ties = jnp.stack([tie_sources[param_index] for param_index in row_params])
    norm_bank_grad = jnp.where(
        slot_ids[:, None, None] == norm_ties[None, :, None], norm_grad[None], 0.0
    )
    head_bank_grad = jnp.where((slot_ids == tie_sources[3])[:, None, None], bias_grad[None], 0.0)
    hidden_bank_grad = jnp.where((slot_ids == tie_sources[9])[:, None], fc_bias_grad[None], 0.0)
    new_norm_momentum = vector_decay * norm_momentum + norm_bank_grad
    new_norm_vectors = norm_vectors - rate * new_norm_momentum
    new_head_bias_momentum = vector_decay * head_bias_momentum + head_bank_grad
    new_head_bias = head_bias - rate * new_head_bias_momentum
    new_fc_bias_momentum = vector_decay * fc_bias_momentum + hidden_bank_grad
    new_fc_bias = fc_bias - rate * new_fc_bias_momentum

    chosen_own = newton_call(
        all_kernel,
        [gate(chosen_pieces[0], kept_updates, block_output)]
        + chosen_pieces[1:],
        own_shape,
        *whole_shape,
        14,
        [pltpu.VMEM(whole_shape, bf16)],
    )
    chosen_updates = returned(chosen_own, shard_rows)
    made = out_call(
        weight_out_kernel,
        tie_sources,
        [chosen_updates, kept_updates, *weight_banks, *average_banks],
        weight_banks + average_banks,
        "weight_out",
    )
    results = []
    for kind in range(KINDS):
        results += [
            bank_rows(kind, bank)
            for bank in (made[kind], new_moments[kind], made[KINDS + kind])
        ]
    return (
        block_output,
        input_grad,
        *results,
        new_norm_vectors,
        new_norm_momentum,
        new_head_bias,
        new_head_bias_momentum,
        new_fc_bias,
        new_fc_bias_momentum,
    )


def solution(mesh):
    dp_count, tensor_count = mesh.devices.shape
    grid = Mesh(
        mesh.devices.reshape(KINDS, dp_count // KINDS, tensor_count), ("plane", "lane", "tensor")
    )
    token_spec = P(DP, None)
    attn_spec = P(None, DP, None, "tensor")
    side_spec = P(None, "tensor", DP)
    fc_spec = P(None, DP, "tensor")
    bank_specs = (attn_spec,) * 3 + (side_spec,) * 3 + (fc_spec,) * 3 + (side_spec,) * 3
    vector_specs = (P(),) * 2 + (P(None, None, "tensor"),) * 2 + (P(None, "tensor"),) * 2
    return jax.shard_map(
        per_device,
        mesh=grid,
        in_specs=(token_spec, token_spec, P()) + bank_specs + vector_specs,
        out_specs=(token_spec, token_spec) + bank_specs + vector_specs,
        check_vma=False,
    )
```

```python
import functools
import math

import jax
import jax.numpy as jnp
from jax import lax
from jax.experimental import pallas as pl
from jax.experimental.pallas import tpu as pltpu
from jax.sharding import Mesh, PartitionSpec as P

D = 768
HEAD = 64
FF = 3072
LEN = 1024
NS_STEPS = 5
KINDS = 4


norm_epsilon = 1e-05
gelu_scale = 0.7978845608028654
coef_one = 3.4445
coef_three = -4.775
coef_five = 2.0315
row_params = (0, 1, 6, 7, 5, 11)
matrix_params = (2, 4, 8, 10)
PACKED = (2, 3, 1, 0)
update_factors = tuple(math.sqrt(columns / D) for columns in (3 * D, D, FF, FF))
vector_decay = 0.9
matrix_decay = 0.5
average_decay = 0.75
DP = ("plane", "lane")
f32 = jnp.float32
bf16 = jnp.bfloat16
PAIR = 128
TILE = 256
NT = (((1,), (1,)), ((), ()))
NN = (((1,), (0,)), ((), ()))


def layer_norm(values, gain_row, shift_row):
    centre = jnp.mean(values, axis=-1, keepdims=True)
    centred = values - centre
    spread = jnp.mean(centred * centred, axis=-1, keepdims=True)
    inverse = lax.rsqrt(spread + norm_epsilon)
    normed = centred * inverse
    return (normed * gain_row + shift_row, normed, inverse)


def norm_backward(grad_out, normed, inverse, gain_row):
    scaled = grad_out * gain_row
    row_inner = jnp.mean(scaled, axis=-1, keepdims=True)
    row_cross = jnp.mean(scaled * normed, axis=-1, keepdims=True)
    grad_in = inverse * (scaled - row_inner - normed * row_cross)
    return (grad_in, jnp.sum(grad_out * normed, axis=0), jnp.sum(grad_out, axis=0))


def product(left, right, dims=NN):
    return lax.dot_general(left, right, dims, preferred_element_type=f32)


def head_lanes(shape, axis, head):
    lane = lax.broadcasted_iota(jnp.int32, shape, axis)
    return (lane < HEAD) if head == 0 else (lane >= HEAD)


def causal(tile):
    key = lax.broadcasted_iota(jnp.int32, (tile, tile), 0)
    query = lax.broadcasted_iota(jnp.int32, (tile, tile), 1)
    return key <= query


def attend_kernel(query_ref, key_ref, value_ref, mixed_ref, total_ref):
    length = query_ref.shape[0]
    tile = min(TILE, length)
    value_t = value_ref[...].T
    keep = causal(tile)
    zero = jnp.zeros((), bf16)
    value_heads = [
        jnp.where(head_lanes(value_t.shape, 0, head), value_t, zero) for head in range(2)
    ]
    for first in range(0, length, tile):
        query = query_ref[first : first + tile, :] * jnp.asarray(HEAD**-0.5, bf16)
        mixed_t = jnp.zeros((PAIR, tile), f32)
        for head in range(2):
            query_head = jnp.where(head_lanes(query.shape, 1, head), query, zero)
            scores = []
            for at in range(0, first + tile, tile):
                score = product(key_ref[at : at + tile, :], query_head, NT)
                scores.append(jnp.where(keep, score, -1e30) if at == first else score)
            top = functools.reduce(
                jnp.maximum, [jnp.max(score, axis=0, keepdims=True) for score in scores]
            )
            weights = [jnp.exp(score - top) for score in scores]
            total = functools.reduce(
                jnp.add, [jnp.sum(weight, axis=0, keepdims=True) for weight in weights]
            )
            inverse = 1.0 / total
            for index, weight in enumerate(weights):
                at = index * tile
                mixed_t += product(
                    value_heads[head][:, at : at + tile], (weight * inverse).astype(bf16)
                )
            total_ref[0, head : head + 1, first : first + tile] = top + jnp.log(total)
        mixed_ref[first : first + tile, :] = mixed_t.T.astype(bf16)


def attend(triple, pair, pairs):
    length = triple.shape[0]

    def column(kind):
        return pl.BlockSpec((length, PAIR), lambda step: (0, kind * pairs + pair))

    return pl.pallas_call(
        attend_kernel,
        grid=(1,),
        in_specs=[column(0), column(1), column(2)],
        out_specs=[
            pl.BlockSpec((length, PAIR), lambda step: (0, 0)),
            pl.BlockSpec((1, 2, length), lambda step: (0, 0, 0)),
        ],
        out_shape=[
            jax.ShapeDtypeStruct((length, PAIR), bf16),
            jax.ShapeDtypeStruct((1, 2, length), f32),
        ],
        compiler_params=pltpu.CompilerParams(vmem_limit_bytes=40 << 20),
        cost_estimate=pl.CostEstimate(
            flops=8 * length * length * PAIR,
            bytes_accessed=8 * length * PAIR,
            transcendentals=length * length,
        ),
        name="attend",
    )(triple, triple, triple)


def attend_back_kernel(
    side_ref,
    query_ref,
    key_ref,
    value_ref,
    grad0_ref,
    grad1_ref,
    input_ref,
    turned0_ref,
    turned1_ref,
    *refs,
):
    pairs = (len(refs) - 7) // 2
    out_ref, kept_ref, sent_ref, key_acc, value_acc, total_ref, mixed_ref = refs[2 * pairs :]
    for pair in range(pairs):

        @pl.when(pl.program_id(0) == pair)
        def _():
            total_ref[...] = refs[pair][...]
            mixed_ref[...] = refs[pairs + pair][...]

    length = query_ref.shape[0]
    tile = min(TILE, length)
    key_t = key_ref[...].T
    keep = causal(tile)
    zero = jnp.zeros((), bf16)
    scale = HEAD**-0.5
    key_heads = [jnp.where(head_lanes(key_t.shape, 0, head), key_t, zero) for head in range(2)]
    for first in range(0, length, tile):
        query = query_ref[first : first + tile, :] * jnp.asarray(scale, bf16)
        middle = grad0_ref.shape[0]
        if first < middle:
            grad = grad0_ref[first : first + tile, :]
        else:
            grad = grad1_ref[first - middle : first - middle + tile, :]
        query_grad_t = jnp.zeros((PAIR, tile), f32)
        key_parts = [None] * (first // tile + 1)
        value_parts = [None] * (first // tile + 1)
        for head in range(2):
            query_head = jnp.where(head_lanes(query.shape, 1, head), query, zero)
            grad_head = jnp.where(head_lanes(grad.shape, 1, head), grad, zero)
            total = total_ref[0, head : head + 1, first : first + tile]
            weights, weight_grads = [], []
            inner = jnp.zeros((1, tile), f32)
            for at in range(0, first + tile, tile):
                score = product(key_ref[at : at + tile, :], query_head, NT)
                weight = jnp.exp(score - total)
                if at == first:
                    weight = jnp.where(keep, weight, 0.0)
                weight_grad = product(value_ref[at : at + tile, :], grad_head, NT)
                inner += jnp.sum(weight * weight_grad, axis=0, keepdims=True)
                weights.append(weight)
                weight_grads.append(weight_grad)
            for index in range(first // tile + 1):
                at = index * tile
                score_grad = (weights[index] * (weight_grads[index] - inner)).astype(bf16)
                query_grad_t += product(key_heads[head][:, at : at + tile], score_grad)
                key_part = product(score_grad, query_head)
                value_part = product(weights[index].astype(bf16), grad_head)
                key_parts[index] = key_part if head == 0 else key_parts[index] + key_part
                value_parts[index] = value_part if head == 0 else value_parts[index] + value_part
        for index in range(first // tile + 1):
            at = index * tile
            if index == first // tile:
                key_acc[at : at + tile, :] = key_parts[index]
                value_acc[at : at + tile, :] = value_parts[index]
            else:
                key_acc[at : at + tile, :] += key_parts[index]
                value_acc[at : at + tile, :] += value_parts[index]
        out_ref[0, first : first + tile, :] = (query_grad_t * scale).T.astype(bf16)
    out_ref[1] = key_acc[...].astype(bf16)
    out_ref[2] = value_acc[...].astype(bf16)
    weights = jnp.concatenate(
        [
            product(
                input_ref[...], jnp.concatenate([out_ref[0], out_ref[1], out_ref[2]], axis=1)
            ),
            product(turned0_ref[...], mixed_ref[:middle, :])
            + product(turned1_ref[...], mixed_ref[middle:, :]),
        ],
        axis=1,
    )
    rows = kept_ref.shape[1]
    is_even = side_ref[0] == 0
    for group in range(kept_ref.shape[0]):
        even = weights[2 * group * rows : (2 * group + 1) * rows]
        odd = weights[(2 * group + 1) * rows : (2 * group + 2) * rows]
        kept_ref[group] = jnp.where(is_even, even, odd).astype(bf16)
        sent_ref[group] = jnp.where(is_even, odd, even).astype(bf16)


def attend_back(triple, mixed_grad, totals, turned_in, turned_mid, mixed, pairs, shard_rows):
    length = triple.shape[0]
    width = turned_in.shape[0]

    def column(kind):
        return pl.BlockSpec((length, PAIR), lambda pair: (0, kind * pairs + pair))

    half = pl.BlockSpec((length // 2, PAIR), lambda pair: (0, pair))
    turned = pl.BlockSpec((width, length // 2), lambda pair: (0, 0))
    groups = width // (2 * shard_rows)
    half_rows = pl.BlockSpec((groups, shard_rows, 4 * PAIR), lambda pair: (0, 0, pair))
    half_shape = jax.ShapeDtypeStruct((groups, shard_rows, 4 * pairs * PAIR), bf16)
    core = (lax.axis_index("lane") & 1).astype(jnp.int32).reshape(1)
    return pl.pallas_call(
        attend_back_kernel,
        grid=(pairs,),
        in_specs=[
            pl.BlockSpec(memory_space=pltpu.SMEM),
            column(0),
            column(1),
            column(2),
            half,
            half,
            pl.BlockSpec((width, length), lambda pair: (0, 0)),
            turned,
            turned,
        ]
        + [pl.BlockSpec((1, 2, length), lambda pair: (0, 0, 0))] * pairs
        + [pl.BlockSpec((length, PAIR), lambda pair: (0, 0))] * pairs,
        out_specs=[
            pl.BlockSpec((3, length, PAIR), lambda pair: (0, 0, pair)),
            half_rows,
            half_rows,
        ],
        out_shape=[
            jax.ShapeDtypeStruct((3, length, pairs * PAIR), bf16),
            half_shape,
            half_shape,
        ],
        scratch_shapes=[
            pltpu.VMEM((length, PAIR), f32),
            pltpu.VMEM((length, PAIR), f32),
            pltpu.VMEM((1, 2, length), f32),
            pltpu.VMEM((length, PAIR), bf16),
        ],
        compiler_params=pltpu.CompilerParams(vmem_limit_bytes=60 << 20),
        cost_estimate=pl.CostEstimate(
            flops=64 * pairs * length * length * PAIR,
            bytes_accessed=30 * pairs * length * PAIR,
            transcendentals=pairs * length * length,
        ),
        name="attend_back",
    )(core, triple, triple, triple, *mixed_grad, turned_in, *turned_mid, *totals, *mixed)


def gram_into(rows_ref, total_ref):
    size = rows_ref.shape[0]
    for at in range(0, size, TILE):
        total_ref[at:, at : at + TILE] = product(rows_ref[at:, :], rows_ref[at : at + TILE, :], NT)
    mirror(total_ref)


def mirror(total_ref):
    size = total_ref.shape[0]
    for at in range(0, size, TILE):
        for low in range(at + TILE, size, TILE):
            total_ref[at : at + TILE, low : low + TILE] = total_ref[
                low : low + TILE, at : at + TILE
            ].T


def identity(rows, columns):
    return lax.broadcasted_iota(jnp.int32, (rows, columns), 0) == lax.broadcasted_iota(
        jnp.int32, (rows, columns), 1
    )


def symmetric_product(left, right, total_ref):
    size = left.shape[0]
    for at in range(0, size, TILE):
        total_ref[at:, at : at + TILE] = product(left[at:], right[:, at : at + TILE])
    mirror(total_ref)
    return total_ref[...]


def with_linear(gram_low, square):
    mixing = coef_three * gram_low.astype(f32) + coef_five * square
    return jnp.where(identity(*mixing.shape), mixing + coef_one, mixing).astype(bf16)


def mixing_of(gram_low, total_ref):
    return with_linear(gram_low, symmetric_product(gram_low, gram_low, total_ref))


def grow(source_ref, made_ref, mixing, factor=None):
    width = source_ref.shape[1]
    chunk = 512 if width % 512 == 0 else width

    @pl.loop(0, width // chunk)
    def _(step):
        span = pl.ds(pl.multiple_of(step * chunk, chunk), chunk)
        grown = product(mixing, source_ref[:, span])
        made_ref[:, span] = (grown if factor is None else grown * factor).astype(bf16)


def next_gram(gram_low, mixing, total_ref):
    half = product(mixing, gram_low).astype(bf16)
    return symmetric_product(half, mixing, total_ref).astype(bf16)


def assemble(piece_refs, rows_ref):
    rows, span = piece_refs[0].shape[1:]
    for core in range(2):
        low, low_other, high, high_other = piece_refs[4 * core : 4 * core + 4]
        for row in range(2):
            at = (2 * core + row) * rows
            row_high = high if row == 0 else high_other
            rows_ref[at : at + rows, :span] = low[row]
            rows_ref[at : at + rows, span : 2 * span] = row_high[0]
            rows_ref[at : at + rows, 2 * span : 3 * span] = low_other[row]
            rows_ref[at : at + rows, 3 * span :] = row_high[1]


def first_rounds(rows_ref, total_ref):
    size = rows_ref.shape[0]
    gram_into(rows_ref, total_ref)
    diagonal = jnp.zeros((TILE, TILE), f32)
    on_diagonal = identity(TILE, TILE)
    for at in range(0, size, TILE):
        diagonal += jnp.where(on_diagonal, total_ref[at : at + TILE, at : at + TILE], 0.0)
    trace = jnp.sum(jnp.sum(diagonal, axis=0, keepdims=True), axis=1, keepdims=True)
    factor = lax.rsqrt(trace + 1e-07)
    gram_low = (total_ref[...] * factor * factor).astype(bf16)
    mixing = mixing_of(gram_low, total_ref)
    so_far = mixing
    for unused_round in range(2):
        gram_low = next_gram(gram_low, mixing, total_ref)
        mixing = mixing_of(gram_low, total_ref)
        so_far = symmetric_product(mixing, so_far, total_ref).astype(bf16)
    grow(rows_ref, rows_ref, so_far, factor)


def last_rounds(rows_ref, own_ref, total_ref):
    own_rows, own_columns = own_ref.shape
    gram_into(rows_ref, total_ref)
    gram_low = total_ref[...].astype(bf16)
    fourth = mixing_of(gram_low, total_ref)
    gram_low = next_gram(gram_low, fourth, total_ref)
    top = gram_low[:own_rows]
    fifth = with_linear(top, product(top, gram_low))
    both = product(fifth, fourth).astype(bf16)
    own_ref[...] = product(both, rows_ref[:, :own_columns]).astype(bf16)


def first_kernel(*refs):
    *piece_refs, rows_ref, total_ref = refs
    assemble(piece_refs, rows_ref)
    first_rounds(rows_ref, total_ref)


def last_kernel(rows_ref, own_ref, total_ref):
    last_rounds(rows_ref, own_ref, total_ref)


def all_kernel(*refs):
    *piece_refs, own_ref, rows_ref, total_ref = refs
    assemble(piece_refs, rows_ref)
    first_rounds(rows_ref, total_ref)
    last_rounds(rows_ref, own_ref, total_ref)


def newton_call(kernel, operands, out_shape, size, width, work, scratch=()):
    return pl.pallas_call(
        kernel,
        in_specs=[pl.BlockSpec(memory_space=pltpu.VMEM)] * len(operands),
        out_specs=pl.BlockSpec(memory_space=pltpu.VMEM),
        out_shape=jax.ShapeDtypeStruct(out_shape, bf16),
        scratch_shapes=[*scratch, pltpu.VMEM((size, size), f32)],
        compiler_params=pltpu.CompilerParams(vmem_limit_bytes=60 << 20),
        cost_estimate=pl.CostEstimate(
            flops=work * size * size * width, bytes_accessed=4 * size * width, transcendentals=0
        ),
        name="newton",
    )(*operands)


def swap_tensor(block):
    return lax.ppermute(block, "tensor", [(0, 1), (1, 0)])


def swap_lane(block, bit):
    count = lax.axis_size("lane")
    return lax.ppermute(block, "lane", [(lane, lane ^ (1 << bit)) for lane in range(count)])


def rows_swapped(block, bit):
    return jnp.concatenate([block, swap_lane(block, bit)], axis=0)


def gate(value, *others):
    count = len(others)

    def kernel(*refs):
        del refs

    anywhere = pl.BlockSpec(memory_space=pl.ANY)
    return pl.pallas_call(
        kernel,
        in_specs=[anywhere] * (count + 1),
        out_specs=anywhere,
        out_shape=jax.ShapeDtypeStruct(value.shape, value.dtype),
        input_output_aliases={0: 0},
        cost_estimate=pl.CostEstimate(flops=0, bytes_accessed=0, transcendentals=0),
        name="gate",
    )(value, *others)


def normed_rows(values):
    centred = values - jnp.mean(values, axis=-1, keepdims=True)
    inverse = lax.rsqrt(jnp.mean(centred * centred, axis=-1, keepdims=True) + norm_epsilon)
    return centred * inverse, inverse


def mlp_kernel(
    side_ref,
    token_ref,
    own0_ref,
    own1_ref,
    own2_ref,
    other0_ref,
    other1_ref,
    other2_ref,
    own_proj_ref,
    other_proj_ref,
    fc_ref,
    out_ref,
    norm_ref,
    bias_ref,
    grad_ref,
    mid_ref,
    in_ref,
    act_ref,
    hidden_grad_ref,
    back_ref,
    part_ref,
    sum_ref,
    back_acc,
    part_acc,
):
    step = pl.program_id(0)

    @pl.when(step == 0)
    def _():
        is_low = side_ref[0] == 0
        own, other = own_proj_ref[...], other_proj_ref[...]
        proj = jnp.concatenate(
            [jnp.where(is_low, own, other), jnp.where(is_low, other, own)], axis=1
        )
        own = jnp.concatenate([own0_ref[...], own1_ref[...], own2_ref[...]], axis=1)
        other = jnp.concatenate([other0_ref[...], other1_ref[...], other2_ref[...]], axis=1)
        mixed = jnp.concatenate(
            [jnp.where(is_low, own, other), jnp.where(is_low, other, own)], axis=1
        )
        mid = token_ref[...].astype(f32) + (product(mixed, proj, NT) + norm_ref[4:5, :])
        mid_ref[...] = mid
        normed, inverse = normed_rows(mid)
        in_ref[...] = (normed * norm_ref[2:3, :] + norm_ref[3:4, :]).astype(bf16)

    fc_part, out_part = fc_ref[...], out_ref[...]
    values = product(in_ref[...], fc_part) + bias_ref[...]
    square = values * values
    curve = jnp.tanh(gelu_scale * (values + 0.044715 * values * square))
    gate_up = 0.5 * (1.0 + curve)
    act = (values * gate_up).astype(bf16)
    act_ref[...] = act
    slope = gate_up + (0.5 * gelu_scale) * values * (1.0 - curve * curve) * (
        1.0 + (3.0 * 0.044715) * square
    )
    hidden_grad = (product(grad_ref[...], out_part) * slope).astype(bf16)
    hidden_grad_ref[...] = hidden_grad
    sum_ref[...] = jnp.sum(hidden_grad.astype(f32), axis=0, keepdims=True)
    back = product(hidden_grad, fc_part, NT)
    part = product(act, out_part, NT)

    @pl.when(step == 0)
    def _():
        back_acc[...] = back
        part_acc[...] = part

    @pl.when(step > 0)
    def _():
        back_acc[...] += back
        part_acc[...] += part

    @pl.when(step == pl.num_programs(0) - 1)
    def _():
        back_ref[...] = back_acc[...].astype(bf16)
        part_ref[...] = part_acc[...].astype(bf16)


def mlp(side, tokens, own, other, full, norm_rows, hidden_bias, grads, chunk, chunks):
    rows, width = tokens.shape
    hidden = hidden_bias.shape[1]
    half = PAIR * len(own)
    part_rows = rows // chunks
    steps = 3
    span = hidden // steps

    def tall(columns):
        return pl.BlockSpec((part_rows, columns), lambda step: (chunk, 0))

    def fixed(shape, column=0):
        return pl.BlockSpec(shape, lambda step: (0, column))

    def moving(size, first=0):
        return pl.BlockSpec((size, span), lambda step: (0, first + step))

    return pl.pallas_call(
        mlp_kernel,
        grid=(steps,),
        in_specs=[pl.BlockSpec(memory_space=pltpu.SMEM), tall(width)]
        + [tall(PAIR)] * 6
        + [
            fixed((width, half), 2 * hidden // half),
            fixed((width, half), full.shape[1] // half - 1),
            moving(width),
            moving(width, steps),
            fixed((6, width)),
            moving(1),
            tall(width),
        ],
        out_specs=[
            fixed((part_rows, width)),
            fixed((part_rows, width)),
            moving(part_rows),
            moving(part_rows),
            fixed((part_rows, width)),
            fixed((part_rows, width)),
            moving(1),
        ],
        out_shape=[
            jax.ShapeDtypeStruct((part_rows, width), f32),
            jax.ShapeDtypeStruct((part_rows, width), bf16),
            jax.ShapeDtypeStruct((part_rows, hidden), bf16),
            jax.ShapeDtypeStruct((part_rows, hidden), bf16),
            jax.ShapeDtypeStruct((part_rows, width), bf16),
            jax.ShapeDtypeStruct((part_rows, width), bf16),
            jax.ShapeDtypeStruct((1, hidden), f32),
        ],
        scratch_shapes=[pltpu.VMEM((part_rows, width), f32), pltpu.VMEM((part_rows, width), f32)],
        compiler_params=pltpu.CompilerParams(vmem_limit_bytes=60 << 20),
        cost_estimate=pl.CostEstimate(
            flops=10 * part_rows * width * hidden,
            bytes_accessed=4 * width * hidden + 20 * part_rows * width,
            transcendentals=part_rows * hidden,
        ),
        name="mlp",
    )(side, tokens, *own, *other, full, full, full, full, norm_rows, hidden_bias, grads)


def weight_kernel(in0_ref, in1_ref, grad_ref, hidden0_ref, hidden1_ref, act0_ref, act1_ref, made_ref, turned_ref):
    step = pl.program_id(0)
    half = pl.num_programs(0) // 2
    rows = in0_ref.shape[0]

    @pl.when(step == 0)
    def _():
        turned_ref[:, :rows] = in0_ref[...].T
        turned_ref[:, rows:] = in1_ref[...].T

    @pl.when(step == half)
    def _():
        turned_ref[...] = grad_ref[...].T

    @pl.when(step < half)
    def _():
        made_ref[...] = product(
            turned_ref[...], jnp.concatenate([hidden0_ref[...], hidden1_ref[...]], axis=0)
        ).astype(bf16)

    @pl.when(step >= half)
    def _():
        made_ref[...] = product(
            turned_ref[...], jnp.concatenate([act0_ref[...], act1_ref[...]], axis=0)
        ).astype(bf16)


def weight_grads(mlp_in, grads, hidden_grad, act):
    rows, width = mlp_in[0].shape
    hidden = act[0].shape[1]
    span = hidden // 3
    whole = pl.BlockSpec((rows, width), lambda step: (0, 0))
    early = pl.BlockSpec((rows, span), lambda step: (0, jnp.minimum(step, 2)))
    late = pl.BlockSpec((rows, span), lambda step: (0, jnp.maximum(step - 3, 0)))
    return pl.pallas_call(
        weight_kernel,
        grid=(6,),
        in_specs=[whole, whole, pl.BlockSpec((2 * rows, width), lambda step: (0, 0))]
        + [early] * 2
        + [late] * 2,
        out_specs=pl.BlockSpec((width, span), lambda step: (0, step)),
        out_shape=jax.ShapeDtypeStruct((width, 2 * hidden), bf16),
        scratch_shapes=[pltpu.VMEM((width, 2 * rows), bf16)],
        compiler_params=pltpu.CompilerParams(vmem_limit_bytes=60 << 20),
        cost_estimate=pl.CostEstimate(
            flops=8 * rows * width * hidden,
            bytes_accessed=8 * rows * hidden + 4 * width * hidden,
            transcendentals=0,
        ),
        name="weight_grads",
    )(*mlp_in, grads, *hidden_grad, *act)


def middle_kernel(own_ref, other_ref, mid_ref, grad_ref, norm_ref, proj_ref, e1_ref, turned_ref, mixed_ref, sum_ref):
    @pl.when(pl.program_id(0) == 0)
    def _():
        sum_ref[...] = jnp.zeros_like(sum_ref)

    back = own_ref[...].astype(f32) + other_ref[...].astype(f32)
    grad = grad_ref[...].astype(f32)
    normed, inverse = normed_rows(mid_ref[...])
    scaled = back * norm_ref[2:3, :]
    inner = jnp.mean(scaled, axis=-1, keepdims=True)
    cross = jnp.mean(scaled * normed, axis=-1, keepdims=True)
    e1 = grad + inverse * (scaled - inner - normed * cross)
    e1_ref[...] = e1
    low = e1.astype(bf16)
    turned_ref[...] = low.T
    mixed_ref[...] = product(low, proj_ref[...]).astype(bf16)
    for row, term in enumerate((back * normed, back, e1, grad)):
        sum_ref[row : row + 1, :] += jnp.sum(term, axis=0, keepdims=True)


def middle(own, other, mid, grads, norm_rows, full, half, chunk):
    rows, width = own.shape
    tile = min(TILE, rows)
    steps = rows // tile
    column = full.shape[1] // half - 2
    plain = pl.BlockSpec((tile, width), lambda step: (step, 0))
    return pl.pallas_call(
        middle_kernel,
        grid=(steps,),
        in_specs=[
            plain,
            plain,
            plain,
            pl.BlockSpec((tile, width), lambda step: (chunk * steps + step, 0)),
            pl.BlockSpec((6, width), lambda step: (0, 0)),
            pl.BlockSpec((width, half), lambda step: (0, column)),
        ],
        out_specs=[
            plain,
            pl.BlockSpec((width, tile), lambda step: (0, step)),
            pl.BlockSpec((tile, half), lambda step: (step, 0)),
            pl.BlockSpec((4, width), lambda step: (0, 0)),
        ],
        out_shape=[
            jax.ShapeDtypeStruct((rows, width), f32),
            jax.ShapeDtypeStruct((width, rows), bf16),
            jax.ShapeDtypeStruct((rows, half), bf16),
            jax.ShapeDtypeStruct((4, width), f32),
        ],
        compiler_params=pltpu.CompilerParams(vmem_limit_bytes=60 << 20),
        cost_estimate=pl.CostEstimate(
            flops=2 * rows * width * half, bytes_accessed=18 * rows * width, transcendentals=0
        ),
        name="middle",
    )(own, other, mid, grads, norm_rows, full)


def bank_rows(kind, bank):
    if kind == 0:
        return bank.transpose(0, 2, 1, 3)
    return bank if kind == 2 else jnp.swapaxes(bank, 1, 2)


def rows_of(kind, ref, slot=0):
    if kind == 0:
        return jnp.concatenate([ref[slot, part] for part in range(3)], axis=1)
    return ref[slot]


def pack_kernel(tie_ref, *refs, scale, padded, kinds):
    del tie_ref
    *bank_refs, made_ref = refs
    at = 0
    for kind, ref in zip(kinds, bank_refs):
        rows = rows_of(kind, ref) * scale
        width = rows.shape[1]
        if padded:
            made_ref[kind] = jnp.zeros(made_ref.shape[1:], made_ref.dtype)
            made_ref[kind, :, :width] = rows.astype(made_ref.dtype)
        else:
            made_ref[:, at : at + width] = rows.astype(made_ref.dtype)
        at += width


def pack(tie_sources, banks, other, scale, kind_of, padded=0, kinds=PACKED):
    def spec(kind):
        param = matrix_params[kind]

        def index(step, tie_ref):
            slot = tie_ref[param]
            return (1 - slot if other else slot,) + (0,) * (banks[kind].ndim - 1)

        return pl.BlockSpec((1,) + banks[kind].shape[1:], index)

    shard_rows = banks[0].shape[2]
    width = sum(banks[kind][0].size // shard_rows for kind in kinds)
    shape = (KINDS, shard_rows, padded) if padded else (shard_rows, width)
    return pl.pallas_call(
        functools.partial(pack_kernel, scale=scale, padded=padded, kinds=kinds),
        grid_spec=pltpu.PrefetchScalarGridSpec(
            num_scalar_prefetch=1,
            grid=(1,),
            in_specs=[spec(kind) for kind in kinds],
            out_specs=pl.BlockSpec(shape, lambda step, tie_ref: (0,) * len(shape)),
        ),
        out_shape=jax.ShapeDtypeStruct(shape, kind_of),
        compiler_params=pltpu.CompilerParams(vmem_limit_bytes=60 << 20),
        cost_estimate=pl.CostEstimate(
            flops=0, bytes_accessed=16 * shard_rows * width, transcendentals=0
        ),
        name="pack",
    )(tie_sources, *[banks[kind] for kind in kinds])


def collect_kernel(first_ref, low_ref, high_ref, triple_ref, hidden0_ref, hidden1_ref, made_ref):
    width = made_ref.shape[1]
    half = triple_ref.shape[2]
    made_ref[0:2, :] = first_ref[...]
    made_ref[2:6, :] = low_ref[...] + high_ref[...]
    made_ref[6:7, :half] = jnp.sum(triple_ref[0].astype(f32), axis=0, keepdims=True)
    made_ref[6:7, half:] = jnp.sum(triple_ref[2].astype(f32), axis=0, keepdims=True)
    for row in range(2):
        span = slice(row * width, (row + 1) * width)
        made_ref[7 + row : 8 + row, :] = hidden0_ref[:, span] + hidden1_ref[:, span]


def collect(*terms):
    width = terms[0].shape[1]
    return pl.pallas_call(
        collect_kernel,
        in_specs=[pl.BlockSpec(memory_space=pltpu.VMEM)] * len(terms),
        out_specs=pl.BlockSpec(memory_space=pltpu.VMEM),
        out_shape=jax.ShapeDtypeStruct((9, width), f32),
        compiler_params=pltpu.CompilerParams(vmem_limit_bytes=60 << 20),
        cost_estimate=pl.CostEstimate(flops=0, bytes_accessed=2 * terms[3].size, transcendentals=0),
        name="collect",
    )(*terms)


def momentum_kernel(reduced_ref, second_ref, decayed_ref, rows_ref, sent_ref, *, half, pairs):
    hidden = sent_ref.shape[2]
    reduced = reduced_ref[0].astype(f32)
    for plane in range(1, KINDS):
        reduced += reduced_ref[plane].astype(f32)
    ordered = [
        reduced[:, (4 * pair + part) * PAIR : (4 * pair + part + 1) * PAIR]
        for part in (3, 0, 1, 2)
        for pair in range(pairs)
    ]
    first = jnp.concatenate(ordered, axis=1)
    rows_ref[:, : 2 * hidden] = decayed_ref[:, : 2 * hidden] + second_ref[...].astype(f32)
    rows_ref[:, 2 * hidden :] = decayed_ref[:, 2 * hidden :] + first
    sent_ref[...] = jnp.zeros_like(sent_ref)
    sent_ref[2] = rows_ref[:, :hidden].astype(bf16)
    sent_ref[3] = rows_ref[:, hidden : 2 * hidden].astype(bf16)
    sent_ref[1, :, :half] = rows_ref[:, 2 * hidden : 2 * hidden + half].astype(bf16)
    sent_ref[0, :, : 3 * half] = rows_ref[:, 2 * hidden + half :].astype(bf16)


def new_momentum(reduced, second, decayed, half):
    shard_rows, width = decayed.shape
    hidden = second.shape[1] // 2
    return pl.pallas_call(
        functools.partial(momentum_kernel, half=half, pairs=half // PAIR),
        in_specs=[pl.BlockSpec(memory_space=pltpu.VMEM)] * 3,
        out_specs=[pl.BlockSpec(memory_space=pltpu.VMEM)] * 2,
        out_shape=[
            jax.ShapeDtypeStruct((shard_rows, width), f32),
            jax.ShapeDtypeStruct((KINDS, shard_rows, hidden), bf16),
        ],
        compiler_params=pltpu.CompilerParams(vmem_limit_bytes=60 << 20),
        cost_estimate=pl.CostEstimate(
            flops=0, bytes_accessed=16 * shard_rows * width, transcendentals=0
        ),
        name="new_momentum",
    )(reduced, second, decayed)


def input_grad_kernel(triple_ref, weight_ref, made_ref):
    grads = jnp.concatenate([triple_ref[0], triple_ref[1], triple_ref[2]], axis=1)
    made_ref[...] = product(grads, weight_ref[...], NT).astype(bf16)


def input_grads(triple_grad, full):
    kinds, rows, half = triple_grad.shape
    width = full.shape[0]
    tile = min(2 * TILE, rows)
    return pl.pallas_call(
        input_grad_kernel,
        grid=(rows // tile,),
        in_specs=[
            pl.BlockSpec((kinds, tile, half), lambda step: (0, step, 0)),
            pl.BlockSpec((width, kinds * half), lambda step: (0, 0)),
        ],
        out_specs=pl.BlockSpec((tile, width), lambda step: (step, 0)),
        out_shape=jax.ShapeDtypeStruct((rows, width), bf16),
        compiler_params=pltpu.CompilerParams(vmem_limit_bytes=60 << 20),
        cost_estimate=pl.CostEstimate(
            flops=2 * rows * width * kinds * half, bytes_accessed=8 * rows * width, transcendentals=0
        ),
        name="input_grads",
    )(triple_grad, full)


def finish_kernel(
    token_ref,
    first_ref,
    other_first_ref,
    mid_ref,
    part_ref,
    other_part_ref,
    e1_ref,
    norm_ref,
    *refs,
):
    out_ref, grad_ref, sum_ref = refs[-3:]

    @pl.when(pl.program_id(0) == 0)
    def _():
        sum_ref[...] = jnp.zeros_like(sum_ref)

    out_ref[...] = (
        mid_ref[...]
        + (part_ref[...].astype(f32) + other_part_ref[...].astype(f32) + norm_ref[5:6, :])
    ).astype(bf16)
    back = first_ref[...].astype(f32) + other_first_ref[...].astype(f32)
    normed, inverse = normed_rows(token_ref[...].astype(f32))
    scaled = back * norm_ref[0:1, :]
    inner = jnp.mean(scaled, axis=-1, keepdims=True)
    cross = jnp.mean(scaled * normed, axis=-1, keepdims=True)
    grad_ref[...] = (e1_ref[...] + inverse * (scaled - inner - normed * cross)).astype(bf16)
    for row, term in enumerate((back * normed, back)):
        sum_ref[row : row + 1, :] += jnp.sum(term, axis=0, keepdims=True)


def finish(tokens, first, other_first, mids, parts, other_parts, e1, norm_rows):
    rows, width = tokens.shape
    half = rows // 2
    tile = min(TILE, half)
    steps = half // tile

    def whole(chunk):
        return pl.BlockSpec((tile, width), lambda step: (chunk * steps + step, 0))

    plain = pl.BlockSpec((tile, width), lambda step: (step, 0))
    made, sums = [], []
    for chunk in range(2):
        *made, total = pl.pallas_call(
            finish_kernel,
            grid=(steps,),
            in_specs=[whole(chunk)] * 3
            + [plain] * 4
            + [pl.BlockSpec((6, width), lambda step: (0, 0))]
            + [pl.BlockSpec(memory_space=pl.ANY)] * len(made),
            out_specs=[
                whole(chunk),
                whole(chunk),
                pl.BlockSpec((2, width), lambda step: (0, 0)),
            ],
            out_shape=[
                jax.ShapeDtypeStruct((rows, width), bf16),
                jax.ShapeDtypeStruct((rows, width), bf16),
                jax.ShapeDtypeStruct((2, width), f32),
            ],
            input_output_aliases={8: 0, 9: 1} if made else {},
            compiler_params=pltpu.CompilerParams(vmem_limit_bytes=60 << 20),
            cost_estimate=pl.CostEstimate(
                flops=40 * half * width, bytes_accessed=22 * half * width, transcendentals=0
            ),
            name="finish",
        )(
            tokens,
            first,
            other_first,
            mids[chunk],
            parts[chunk],
            other_parts[chunk],
            e1[chunk],
            norm_rows,
            *made,
        )
        sums.append(total)
    return (*made, sums[0] + sums[1])


def put_rows(kind, ref, slot, rows):
    if kind == 0:
        half = ref.shape[3]
        for part in range(3):
            ref[slot, part] = rows[:, part * half : (part + 1) * half]
    else:
        ref[slot] = rows


def momentum_out_kernel(tie_ref, rows_ref, *refs):
    at = 0
    for kind, bank_ref, made_ref in zip(PACKED, refs[:KINDS], refs[KINDS:]):
        width = bank_ref[0].size // rows_ref.shape[0]
        renewed = rows_ref[:, at : at + width]
        at += width
        for slot in range(bank_ref.shape[0]):
            chosen = tie_ref[matrix_params[kind]] == slot

            @pl.when(chosen)
            def _():
                put_rows(kind, made_ref, slot, renewed)

            @pl.when(jnp.logical_not(chosen))
            def _():
                made_ref[slot] = matrix_decay * bank_ref[slot]


def weight_out_kernel(tie_ref, chosen_ref, kept_ref, *refs):
    weight_refs, average_refs = refs[:KINDS], refs[KINDS : 2 * KINDS]
    new_refs, mean_refs = refs[2 * KINDS : 3 * KINDS], refs[3 * KINDS :]
    for kind in range(KINDS):
        width = weight_refs[kind][0].size // chosen_ref.shape[1]
        for slot in range(weight_refs[kind].shape[0]):
            chosen = tie_ref[matrix_params[kind]] == slot
            rows = jnp.where(chosen, chosen_ref[kind, :, :width], kept_ref[kind, :, :width])
            step = (-update_factors[kind]) * rows.astype(f32)
            new = rows_of(kind, weight_refs[kind], slot) + step
            put_rows(kind, new_refs[kind], slot, new)
            mean = average_decay * rows_of(kind, average_refs[kind], slot)
            put_rows(kind, mean_refs[kind], slot, mean + (1.0 - average_decay) * new)


def out_call(kernel, tie_sources, operands, banks, name):
    inside = pl.BlockSpec(memory_space=pltpu.VMEM)
    size = sum(bank.size for bank in banks)
    return pl.pallas_call(
        kernel,
        in_specs=[pl.BlockSpec(memory_space=pltpu.SMEM)] + [inside] * len(operands),
        out_specs=[inside] * len(banks),
        out_shape=[jax.ShapeDtypeStruct(bank.shape, f32) for bank in banks],
        compiler_params=pltpu.CompilerParams(vmem_limit_bytes=60 << 20),
        cost_estimate=pl.CostEstimate(flops=0, bytes_accessed=12 * size, transcendentals=0),
        name=name,
    )(tie_sources, *operands)


def arrange_kernel(*refs, count):
    *pieces, out_ref = refs
    plane, lane = lax.axis_index("plane"), lax.axis_index("lane")
    for flip, piece in enumerate(pieces):
        for shift in range(KINDS):
            out_ref[lax.rem(plane + KINDS - shift, KINDS) * count + (lane ^ flip)] = piece[shift]


def dp_gather(rows, *sooner):
    count = lax.axis_size("lane")
    size, width = rows.shape
    if size % 16:
        made = lax.all_gather(rows, DP, axis=0, tiled=True)
        return made
    planes = jnp.stack(
            [rows]
            + [
                lax.ppermute(
                    rows, "plane", [(plane, (plane + shift) % KINDS) for plane in range(KINDS)]
                )
                for shift in range(1, KINDS)
            ]
    )
    pieces = [planes]
    order = [0]
    for bit in reversed(range(count.bit_length() - 1)):
        if bit == 0:
            pieces[-1] = gate(pieces[-1], *sooner)
        pieces += [swap_lane(piece, bit) for piece in pieces]
        order += [flip | (1 << bit) for flip in order]
    pieces = [piece for unused_flip, piece in sorted(zip(order, pieces), key=lambda pair: pair[0])]
    made = pl.pallas_call(
        functools.partial(arrange_kernel, count=count),
        in_specs=[pl.BlockSpec(memory_space=pltpu.VMEM)] * count,
        out_specs=pl.BlockSpec(memory_space=pltpu.VMEM),
        out_shape=jax.ShapeDtypeStruct((KINDS * count, size, width), bf16),
        compiler_params=pltpu.CompilerParams(vmem_limit_bytes=60 << 20),
        cost_estimate=pl.CostEstimate(
            flops=0, bytes_accessed=4 * KINDS * count * size * width, transcendentals=0
        ),
        name="arrange",
    )(*pieces)
    return made.reshape(KINDS * count * size, width)


def axis_sum(terms, axis):
    count = lax.axis_size(axis)

    def swapped(flip):
        return lax.ppermute(terms, axis, [(place, place ^ flip) for place in range(count)])

    for bit in range(2, count.bit_length() - 1):
        terms = terms + swapped(1 << bit)
    return (terms + swapped(1)) + (swapped(2) + swapped(3))


def lane_reduce(kept, sent):
    shard_rows, width = kept.shape[1:]
    lane = lax.axis_index("lane")
    lane_bits = lax.axis_size("lane").bit_length() - 1
    stages = []
    for bit in range(lane_bits):
        if bit > 0:
            view = part.reshape(-1, 2, shard_rows, width)
            own_bit = (lane >> bit) & 1
            kept = lax.dynamic_index_in_dim(view, own_bit, 1, keepdims=False)
            sent = lax.dynamic_index_in_dim(view, 1 - own_bit, 1, keepdims=False)
        part = (kept.astype(f32) + swap_lane(sent, bit).astype(f32)).astype(bf16)
        stages.append(part)
    return part.reshape(KINDS, shard_rows, width), stages


def plane_rows(outgoing):
    arrived = lax.all_to_all(outgoing, "plane", split_axis=0, concat_axis=0, tiled=True)
    return arrived.reshape(-1, outgoing.shape[2])


def plane_gather(block, waits=(), last=()):
    lane_bits = lax.axis_size("lane").bit_length() - 1
    if waits and waits[0]:
        block = gate(block, *waits[0])
    for bit in range(2, lane_bits):
        block = rows_swapped(block, bit)
    middle = block.shape[1] // 2
    low, high = block[:, :middle], block[:, middle:]
    low_other, high_other = swap_lane(low, 1), swap_tensor(high)
    if waits:
        low_other, high_other = gate(low_other, *waits[1]), gate(high_other, *waits[1])
    low = jnp.stack([low, low_other])
    high = jnp.stack([high, high_other])
    mine = [low, swap_tensor(low), high, swap_lane(high, 1)]
    if last:
        mine[3] = gate(mine[3], *last)
    return mine + [swap_lane(piece, 0) for piece in mine]


def returned(own, shard_rows):
    own = own[: KINDS * shard_rows].reshape(KINDS, shard_rows, -1)
    return lax.all_to_all(own, "plane", split_axis=0, concat_axis=0, tiled=True)


def per_device(
    tokens,
    cotangent,
    tie_sources,
    attn_weight,
    attn_momentum,
    attn_average,
    proj_weight,
    proj_momentum,
    proj_average,
    fc_weight,
    fc_momentum,
    fc_average,
    out_weight,
    out_momentum,
    out_average,
    norm_vectors,
    norm_momentum,
    head_bias,
    head_bias_momentum,
    fc_bias,
    fc_bias_momentum,
):
    row_count, model_width = tokens.shape
    dp_count = lax.axis_size("plane") * lax.axis_size("lane")
    shard_rows = model_width // dp_count
    half_width = proj_weight.shape[1]
    hidden_half = fc_weight.shape[2]
    widths = (3 * half_width, half_width, hidden_half, hidden_half)
    slot_count = attn_weight.shape[0]

    def choose_slot(bank, param_index):
        return lax.dynamic_index_in_dim(bank, tie_sources[param_index], 0, keepdims=False)

    weight_banks, momentum_banks, average_banks = (
        [bank_rows(kind, bank) for kind, bank in enumerate(banks)]
        for banks in (
            (attn_weight, proj_weight, fc_weight, out_weight),
            (attn_momentum, proj_momentum, fc_momentum, out_momentum),
            (attn_average, proj_average, fc_average, out_average),
        )
    )
    norm_rows = jnp.stack(
        [
            norm_vectors[tie_sources[param_index], row_index]
            for row_index, param_index in enumerate(row_params)
        ]
    )

    attn_rows = pack(tie_sources, weight_banks, False, 1.0, bf16, kinds=PACKED[3:])
    low_rows = pack(tie_sources, weight_banks, False, 1.0, bf16, kinds=PACKED[:3])
    inputs = tokens.astype(f32)
    attn_normed, unused_unit, unused_inverse = layer_norm(inputs, norm_rows[0], norm_rows[1])
    attn_in = attn_normed.astype(bf16)
    turned_in = attn_in.T
    decayed_rows = pack(tie_sources, momentum_banks, False, matrix_decay, f32)
    kept_out = pack(tie_sources, momentum_banks, True, matrix_decay, bf16, hidden_half)
    attn_full = dp_gather(attn_rows, turned_in, decayed_rows, kept_out)
    other_proj_rows = swap_tensor(low_rows[:, 2 * hidden_half :])
    full = lax.all_gather(
        jnp.concatenate([low_rows, other_proj_rows], axis=1),
        DP,
        axis=0,
        tiled=True,
    )
    pairs = half_width // PAIR

    query_bias = choose_slot(head_bias, 3)
    hidden_bias = choose_slot(fc_bias, 9)
    projected = jnp.dot(attn_in, attn_full, preferred_element_type=f32)
    bias_row = jnp.concatenate([query_bias[0], jnp.zeros_like(query_bias[0]), query_bias[1]])
    triple = (projected + bias_row[None]).astype(bf16)
    own_mixed, other_mixed, log_totals = [], [], []
    for pair in range(pairs):
        mixed, totals = attend(triple, pair, pairs)
        own_mixed.append(mixed)
        other_mixed.append(swap_tensor(mixed))
        log_totals.append(totals)

    side = lax.axis_index("tensor").astype(jnp.int32).reshape(1)
    chunk_rows = norm_rows
    made = []
    for chunk in range(2):
        made.append(
            mlp(
                side,
                tokens,
                own_mixed,
                other_mixed,
                full,
                chunk_rows,
                hidden_bias[None],
                cotangent,
                chunk,
                2,
            )
        )
        chunk_rows = gate(norm_rows, made[0][4])
    mids, mlp_in, act, hidden_grad, backs, parts, hidden_terms = zip(*made)
    other_backs = [swap_tensor(back) for back in backs]
    kept_rows = plane_rows(gate(kept_out, full))
    middles = []
    for chunk in range(2):
        other_back = other_backs[chunk]
        if chunk == 1:
            second_part = weight_grads(
                (gate(mlp_in[0], middles[0][0], kept_rows), mlp_in[1]), cotangent, hidden_grad, act
            )
            other_back = gate(other_back, second_part)
        middles.append(
            middle(
                backs[chunk],
                other_back,
                mids[chunk],
                cotangent,
                norm_rows,
                full,
                half_width,
                chunk,
            )
        )
    e1, turned_mid, mixed_grad, middle_terms = zip(*middles)
    second_shard = lax.psum_scatter(second_part, DP, scatter_dimension=0, tiled=True)
    other_parts = [swap_tensor(gate(part, *mixed_grad)) for part in parts]
    kept_pieces = plane_gather(kept_rows, [other_backs[1:], mixed_grad])
    triple_grad, attn_kept, attn_sent = attend_back(
        triple,
        (mixed_grad[0], mixed_grad[1]),
        log_totals,
        turned_in,
        turned_mid,
        own_mixed,
        pairs,
        shard_rows,
    )
    part, stages = lane_reduce(
        attn_kept, gate(attn_sent, kept_pieces[1], kept_pieces[3], other_parts[0])
    )
    first_part = input_grads(triple_grad, attn_full)
    other_first = swap_tensor(first_part)
    whole_shape = (model_width, 2 * hidden_half)
    own_shape = (-(-KINDS * shard_rows // 16) * 16, hidden_half)
    kept_whole = newton_call(
        first_kernel,
        [gate(kept_pieces[0], stages[0])] + kept_pieces[1:],
        whole_shape,
        *whole_shape,
        8,
    )
    first_shard = lax.all_to_all(
        gate(part, kept_whole, *other_parts), "plane", split_axis=0, concat_axis=0, tiled=True
    )
    kept_own = newton_call(
        last_kernel, [gate(kept_whole, stages[-1])], own_shape, *whole_shape, 4
    )
    renewed_rows, outgoing = new_momentum(
        gate(first_shard, other_first, kept_own), second_shard, decayed_rows, half_width
    )
    chosen_rows = plane_rows(outgoing)
    block_output, input_grad, norm_one_terms = finish(
        tokens,
        first_part,
        other_first,
        mids,
        parts,
        other_parts,
        e1,
        gate(norm_rows, renewed_rows),
    )
    collected = collect(norm_one_terms, *middle_terms, triple_grad, *hidden_terms)
    lane_terms = axis_sum(collected, "lane")
    terms = axis_sum(lane_terms, "plane")
    ordered = [momentum_banks[kind] for kind in PACKED]
    new_moments = out_call(
        momentum_out_kernel,
        tie_sources,
        [gate(renewed_rows, lane_terms)] + ordered,
        ordered,
        "momentum_out",
    )
    kept_updates = returned(gate(kept_own, chosen_rows), shard_rows)
    chosen_pieces = plane_gather(
        gate(chosen_rows, collected),
        [(), (lane_terms,)],
        [terms, kept_updates, *new_moments],
    )
    new_moments = [new_moments[PACKED.index(kind)] for kind in range(KINDS)]
    norm_grad = terms[:6]
    bias_grad = terms[6].reshape(2, half_width)
    fc_bias_grad = terms[7:].reshape(hidden_half)

    slot_ids = jnp.arange(slot_count, dtype=jnp.int32)
    rate = 0.1 / math.sqrt(row_count * dp_count)
    norm_ties = jnp.stack([tie_sources[param_index] for param_index in row_params])
    norm_bank_grad = jnp.where(
        slot_ids[:, None, None] == norm_ties[None, :, None], norm_grad[None], 0.0
    )
    head_bank_grad = jnp.where((slot_ids == tie_sources[3])[:, None, None], bias_grad[None], 0.0)
    hidden_bank_grad = jnp.where((slot_ids == tie_sources[9])[:, None], fc_bias_grad[None], 0.0)
    new_norm_momentum = vector_decay * norm_momentum + norm_bank_grad
    new_norm_vectors = norm_vectors - rate * new_norm_momentum
    new_head_bias_momentum = vector_decay * head_bias_momentum + head_bank_grad
    new_head_bias = head_bias - rate * new_head_bias_momentum
    new_fc_bias_momentum = vector_decay * fc_bias_momentum + hidden_bank_grad
    new_fc_bias = fc_bias - rate * new_fc_bias_momentum

    chosen_own = newton_call(
        all_kernel,
        [gate(chosen_pieces[0], block_output)]
        + chosen_pieces[1:],
        own_shape,
        *whole_shape,
        14,
        [pltpu.VMEM(whole_shape, bf16)],
    )
    chosen_updates = returned(chosen_own, shard_rows)
    made = out_call(
        weight_out_kernel,
        tie_sources,
        [chosen_updates, kept_updates, *weight_banks, *average_banks],
        weight_banks + average_banks,
        "weight_out",
    )
    results = []
    for kind in range(KINDS):
        results += [
            bank_rows(kind, bank)
            for bank in (made[kind], new_moments[kind], made[KINDS + kind])
        ]
    return (
        block_output,
        input_grad,
        *results,
        new_norm_vectors,
        new_norm_momentum,
        new_head_bias,
        new_head_bias_momentum,
        new_fc_bias,
        new_fc_bias_momentum,
    )


def solution(mesh):
    dp_count, tensor_count = mesh.devices.shape
    grid = Mesh(
        mesh.devices.reshape(KINDS, dp_count // KINDS, tensor_count), ("plane", "lane", "tensor")
    )
    token_spec = P(DP, None)
    attn_spec = P(None, DP, None, "tensor")
    side_spec = P(None, "tensor", DP)
    fc_spec = P(None, DP, "tensor")
    bank_specs = (attn_spec,) * 3 + (side_spec,) * 3 + (fc_spec,) * 3 + (side_spec,) * 3
    vector_specs = (P(),) * 2 + (P(None, None, "tensor"),) * 2 + (P(None, "tensor"),) * 2
    return jax.shard_map(
        per_device,
        mesh=grid,
        in_specs=(token_spec, token_spec, P()) + bank_specs + vector_specs,
        out_specs=(token_spec, token_spec) + bank_specs + vector_specs,
        check_vma=False,
    )
```

```python
import functools
import math

import jax
import jax.numpy as jnp
from jax import lax
from jax.experimental import pallas as pl
from jax.experimental.pallas import tpu as pltpu
from jax.sharding import Mesh, PartitionSpec as P

D = 768
HEAD = 64
FF = 3072
LEN = 1024
NS_STEPS = 5
KINDS = 4


norm_epsilon = 1e-05
gelu_scale = 0.7978845608028654
coef_one = 3.4445
coef_three = -4.775
coef_five = 2.0315
row_params = (0, 1, 6, 7, 5, 11)
matrix_params = (2, 4, 8, 10)
PACKED = (2, 3, 1, 0)
update_factors = tuple(math.sqrt(columns / D) for columns in (3 * D, D, FF, FF))
vector_decay = 0.9
matrix_decay = 0.5
average_decay = 0.75
DP = ("plane", "lane")
f32 = jnp.float32
bf16 = jnp.bfloat16
PAIR = 128
TILE = 256
NT = (((1,), (1,)), ((), ()))
NN = (((1,), (0,)), ((), ()))


def layer_norm(values, gain_row, shift_row):
    centre = jnp.mean(values, axis=-1, keepdims=True)
    centred = values - centre
    spread = jnp.mean(centred * centred, axis=-1, keepdims=True)
    inverse = lax.rsqrt(spread + norm_epsilon)
    normed = centred * inverse
    return (normed * gain_row + shift_row, normed, inverse)


def norm_backward(grad_out, normed, inverse, gain_row):
    scaled = grad_out * gain_row
    row_inner = jnp.mean(scaled, axis=-1, keepdims=True)
    row_cross = jnp.mean(scaled * normed, axis=-1, keepdims=True)
    grad_in = inverse * (scaled - row_inner - normed * row_cross)
    return (grad_in, jnp.sum(grad_out * normed, axis=0), jnp.sum(grad_out, axis=0))


def product(left, right, dims=NN):
    return lax.dot_general(left, right, dims, preferred_element_type=f32)


def head_lanes(shape, axis, head):
    lane = lax.broadcasted_iota(jnp.int32, shape, axis)
    return (lane < HEAD) if head == 0 else (lane >= HEAD)


def causal(tile):
    key = lax.broadcasted_iota(jnp.int32, (tile, tile), 0)
    query = lax.broadcasted_iota(jnp.int32, (tile, tile), 1)
    return key <= query


def attend_kernel(query_ref, key_ref, value_ref, mixed_ref, total_ref):
    length = query_ref.shape[0]
    tile = min(TILE, length)
    value_t = value_ref[...].T
    keep = causal(tile)
    zero = jnp.zeros((), bf16)
    value_heads = [
        jnp.where(head_lanes(value_t.shape, 0, head), value_t, zero) for head in range(2)
    ]
    for first in range(0, length, tile):
        query = query_ref[first : first + tile, :] * jnp.asarray(HEAD**-0.5, bf16)
        mixed_t = jnp.zeros((PAIR, tile), f32)
        for head in range(2):
            query_head = jnp.where(head_lanes(query.shape, 1, head), query, zero)
            scores = []
            for at in range(0, first + tile, tile):
                score = product(key_ref[at : at + tile, :], query_head, NT)
                scores.append(jnp.where(keep, score, -1e30) if at == first else score)
            top = functools.reduce(
                jnp.maximum, [jnp.max(score, axis=0, keepdims=True) for score in scores]
            )
            weights = [jnp.exp(score - top) for score in scores]
            total = functools.reduce(
                jnp.add, [jnp.sum(weight, axis=0, keepdims=True) for weight in weights]
            )
            inverse = 1.0 / total
            for index, weight in enumerate(weights):
                at = index * tile
                mixed_t += product(
                    value_heads[head][:, at : at + tile], (weight * inverse).astype(bf16)
                )
            total_ref[0, head : head + 1, first : first + tile] = top + jnp.log(total)
        mixed_ref[first : first + tile, :] = mixed_t.T.astype(bf16)


def attend(triple, pair, pairs):
    length = triple.shape[0]

    def column(kind):
        return pl.BlockSpec((length, PAIR), lambda step: (0, kind * pairs + pair))

    return pl.pallas_call(
        attend_kernel,
        grid=(1,),
        in_specs=[column(0), column(1), column(2)],
        out_specs=[
            pl.BlockSpec((length, PAIR), lambda step: (0, 0)),
            pl.BlockSpec((1, 2, length), lambda step: (0, 0, 0)),
        ],
        out_shape=[
            jax.ShapeDtypeStruct((length, PAIR), bf16),
            jax.ShapeDtypeStruct((1, 2, length), f32),
        ],
        compiler_params=pltpu.CompilerParams(vmem_limit_bytes=40 << 20),
        cost_estimate=pl.CostEstimate(
            flops=8 * length * length * PAIR,
            bytes_accessed=8 * length * PAIR,
            transcendentals=length * length,
        ),
        name="attend",
    )(triple, triple, triple)


def attend_back_kernel(
    side_ref,
    query_ref,
    key_ref,
    value_ref,
    grad0_ref,
    grad1_ref,
    input_ref,
    turned0_ref,
    turned1_ref,
    *refs,
):
    pairs = (len(refs) - 7) // 2
    out_ref, kept_ref, sent_ref, key_acc, value_acc, total_ref, mixed_ref = refs[2 * pairs :]
    for pair in range(pairs):

        @pl.when(pl.program_id(0) == pair)
        def _():
            total_ref[...] = refs[pair][...]
            mixed_ref[...] = refs[pairs + pair][...]

    length = query_ref.shape[0]
    tile = min(TILE, length)
    key_t = key_ref[...].T
    keep = causal(tile)
    zero = jnp.zeros((), bf16)
    scale = HEAD**-0.5
    key_heads = [jnp.where(head_lanes(key_t.shape, 0, head), key_t, zero) for head in range(2)]
    for first in range(0, length, tile):
        query = query_ref[first : first + tile, :] * jnp.asarray(scale, bf16)
        middle = grad0_ref.shape[0]
        if first < middle:
            grad = grad0_ref[first : first + tile, :]
        else:
            grad = grad1_ref[first - middle : first - middle + tile, :]
        query_grad_t = jnp.zeros((PAIR, tile), f32)
        key_parts = [None] * (first // tile + 1)
        value_parts = [None] * (first // tile + 1)
        for head in range(2):
            query_head = jnp.where(head_lanes(query.shape, 1, head), query, zero)
            grad_head = jnp.where(head_lanes(grad.shape, 1, head), grad, zero)
            total = total_ref[0, head : head + 1, first : first + tile]
            weights, weight_grads = [], []
            inner = jnp.zeros((1, tile), f32)
            for at in range(0, first + tile, tile):
                score = product(key_ref[at : at + tile, :], query_head, NT)
                weight = jnp.exp(score - total)
                if at == first:
                    weight = jnp.where(keep, weight, 0.0)
                weight_grad = product(value_ref[at : at + tile, :], grad_head, NT)
                inner += jnp.sum(weight * weight_grad, axis=0, keepdims=True)
                weights.append(weight)
                weight_grads.append(weight_grad)
            for index in range(first // tile + 1):
                at = index * tile
                score_grad = (weights[index] * (weight_grads[index] - inner)).astype(bf16)
                query_grad_t += product(key_heads[head][:, at : at + tile], score_grad)
                key_part = product(score_grad, query_head)
                value_part = product(weights[index].astype(bf16), grad_head)
                key_parts[index] = key_part if head == 0 else key_parts[index] + key_part
                value_parts[index] = value_part if head == 0 else value_parts[index] + value_part
        for index in range(first // tile + 1):
            at = index * tile
            if index == first // tile:
                key_acc[at : at + tile, :] = key_parts[index]
                value_acc[at : at + tile, :] = value_parts[index]
            else:
                key_acc[at : at + tile, :] += key_parts[index]
                value_acc[at : at + tile, :] += value_parts[index]
        out_ref[0, first : first + tile, :] = (query_grad_t * scale).T.astype(bf16)
    out_ref[1] = key_acc[...].astype(bf16)
    out_ref[2] = value_acc[...].astype(bf16)
    weights = jnp.concatenate(
        [
            product(
                input_ref[...], jnp.concatenate([out_ref[0], out_ref[1], out_ref[2]], axis=1)
            ),
            product(turned0_ref[...], mixed_ref[:middle, :])
            + product(turned1_ref[...], mixed_ref[middle:, :]),
        ],
        axis=1,
    )
    rows = kept_ref.shape[1]
    is_even = side_ref[0] == 0
    for group in range(kept_ref.shape[0]):
        even = weights[2 * group * rows : (2 * group + 1) * rows]
        odd = weights[(2 * group + 1) * rows : (2 * group + 2) * rows]
        kept_ref[group] = jnp.where(is_even, even, odd).astype(bf16)
        sent_ref[group] = jnp.where(is_even, odd, even).astype(bf16)


def attend_back(triple, mixed_grad, totals, turned_in, turned_mid, mixed, pairs, shard_rows):
    length = triple.shape[0]
    width = turned_in.shape[0]

    def column(kind):
        return pl.BlockSpec((length, PAIR), lambda pair: (0, kind * pairs + pair))

    half = pl.BlockSpec((length // 2, PAIR), lambda pair: (0, pair))
    turned = pl.BlockSpec((width, length // 2), lambda pair: (0, 0))
    groups = width // (2 * shard_rows)
    half_rows = pl.BlockSpec((groups, shard_rows, 4 * PAIR), lambda pair: (0, 0, pair))
    half_shape = jax.ShapeDtypeStruct((groups, shard_rows, 4 * pairs * PAIR), bf16)
    core = (lax.axis_index("lane") & 1).astype(jnp.int32).reshape(1)
    return pl.pallas_call(
        attend_back_kernel,
        grid=(pairs,),
        in_specs=[
            pl.BlockSpec(memory_space=pltpu.SMEM),
            column(0),
            column(1),
            column(2),
            half,
            half,
            pl.BlockSpec((width, length), lambda pair: (0, 0)),
            turned,
            turned,
        ]
        + [pl.BlockSpec((1, 2, length), lambda pair: (0, 0, 0))] * pairs
        + [pl.BlockSpec((length, PAIR), lambda pair: (0, 0))] * pairs,
        out_specs=[
            pl.BlockSpec((3, length, PAIR), lambda pair: (0, 0, pair)),
            half_rows,
            half_rows,
        ],
        out_shape=[
            jax.ShapeDtypeStruct((3, length, pairs * PAIR), bf16),
            half_shape,
            half_shape,
        ],
        scratch_shapes=[
            pltpu.VMEM((length, PAIR), f32),
            pltpu.VMEM((length, PAIR), f32),
            pltpu.VMEM((1, 2, length), f32),
            pltpu.VMEM((length, PAIR), bf16),
        ],
        compiler_params=pltpu.CompilerParams(vmem_limit_bytes=60 << 20),
        cost_estimate=pl.CostEstimate(
            flops=64 * pairs * length * length * PAIR,
            bytes_accessed=30 * pairs * length * PAIR,
            transcendentals=pairs * length * length,
        ),
        name="attend_back",
    )(core, triple, triple, triple, *mixed_grad, turned_in, *turned_mid, *totals, *mixed)


def gram_into(rows_ref, total_ref):
    size = rows_ref.shape[0]
    for at in range(0, size, TILE):
        total_ref[at:, at : at + TILE] = product(rows_ref[at:, :], rows_ref[at : at + TILE, :], NT)
    mirror(total_ref)


def mirror(total_ref):
    size = total_ref.shape[0]
    for at in range(0, size, TILE):
        for low in range(at + TILE, size, TILE):
            total_ref[at : at + TILE, low : low + TILE] = total_ref[
                low : low + TILE, at : at + TILE
            ].T


def identity(rows, columns):
    return lax.broadcasted_iota(jnp.int32, (rows, columns), 0) == lax.broadcasted_iota(
        jnp.int32, (rows, columns), 1
    )


def symmetric_product(left, right, total_ref):
    size = left.shape[0]
    for at in range(0, size, TILE):
        total_ref[at:, at : at + TILE] = product(left[at:], right[:, at : at + TILE])
    mirror(total_ref)
    return total_ref[...]


def with_linear(gram_low, square):
    mixing = coef_three * gram_low.astype(f32) + coef_five * square
    return jnp.where(identity(*mixing.shape), mixing + coef_one, mixing).astype(bf16)


def mixing_of(gram_low, total_ref):
    return with_linear(gram_low, symmetric_product(gram_low, gram_low, total_ref))


def grow(source_ref, made_ref, mixing, factor=None):
    width = source_ref.shape[1]
    chunk = 512 if width % 512 == 0 else width

    @pl.loop(0, width // chunk)
    def _(step):
        span = pl.ds(pl.multiple_of(step * chunk, chunk), chunk)
        grown = product(mixing, source_ref[:, span])
        made_ref[:, span] = (grown if factor is None else grown * factor).astype(bf16)


def next_gram(gram_low, mixing, total_ref):
    half = product(mixing, gram_low).astype(bf16)
    return symmetric_product(half, mixing, total_ref).astype(bf16)


def assemble(piece_refs, rows_ref):
    rows, span = piece_refs[0].shape[1:]
    for core in range(2):
        low, low_other, high, high_other = piece_refs[4 * core : 4 * core + 4]
        for row in range(2):
            at = (2 * core + row) * rows
            row_high = high if row == 0 else high_other
            rows_ref[at : at + rows, :span] = low[row]
            rows_ref[at : at + rows, span : 2 * span] = row_high[0]
            rows_ref[at : at + rows, 2 * span : 3 * span] = low_other[row]
            rows_ref[at : at + rows, 3 * span :] = row_high[1]


def first_rounds(rows_ref, total_ref):
    size = rows_ref.shape[0]
    gram_into(rows_ref, total_ref)
    diagonal = jnp.zeros((TILE, TILE), f32)
    on_diagonal = identity(TILE, TILE)
    for at in range(0, size, TILE):
        diagonal += jnp.where(on_diagonal, total_ref[at : at + TILE, at : at + TILE], 0.0)
    trace = jnp.sum(jnp.sum(diagonal, axis=0, keepdims=True), axis=1, keepdims=True)
    factor = lax.rsqrt(trace + 1e-07)
    gram_low = (total_ref[...] * factor * factor).astype(bf16)
    mixing = mixing_of(gram_low, total_ref)
    so_far = mixing
    for unused_round in range(2):
        gram_low = next_gram(gram_low, mixing, total_ref)
        mixing = mixing_of(gram_low, total_ref)
        so_far = symmetric_product(mixing, so_far, total_ref).astype(bf16)
    grow(rows_ref, rows_ref, so_far, factor)


def last_rounds(rows_ref, own_ref, total_ref):
    own_rows, own_columns = own_ref.shape
    gram_into(rows_ref, total_ref)
    gram_low = total_ref[...].astype(bf16)
    fourth = mixing_of(gram_low, total_ref)
    gram_low = next_gram(gram_low, fourth, total_ref)
    top = gram_low[:own_rows]
    fifth = with_linear(top, product(top, gram_low))
    both = product(fifth, fourth).astype(bf16)
    own_ref[...] = product(both, rows_ref[:, :own_columns]).astype(bf16)


def first_kernel(*refs):
    *piece_refs, rows_ref, total_ref = refs
    assemble(piece_refs, rows_ref)
    first_rounds(rows_ref, total_ref)


def last_kernel(rows_ref, own_ref, total_ref):
    last_rounds(rows_ref, own_ref, total_ref)


def all_kernel(*refs):
    *piece_refs, own_ref, rows_ref, total_ref = refs
    assemble(piece_refs, rows_ref)
    first_rounds(rows_ref, total_ref)
    last_rounds(rows_ref, own_ref, total_ref)


def newton_call(kernel, operands, out_shape, size, width, work, scratch=()):
    return pl.pallas_call(
        kernel,
        in_specs=[pl.BlockSpec(memory_space=pltpu.VMEM)] * len(operands),
        out_specs=pl.BlockSpec(memory_space=pltpu.VMEM),
        out_shape=jax.ShapeDtypeStruct(out_shape, bf16),
        scratch_shapes=[*scratch, pltpu.VMEM((size, size), f32)],
        compiler_params=pltpu.CompilerParams(vmem_limit_bytes=60 << 20),
        cost_estimate=pl.CostEstimate(
            flops=work * size * size * width, bytes_accessed=4 * size * width, transcendentals=0
        ),
        name="newton",
    )(*operands)


def swap_tensor(block):
    return lax.ppermute(block, "tensor", [(0, 1), (1, 0)])


def swap_lane(block, bit):
    count = lax.axis_size("lane")
    return lax.ppermute(block, "lane", [(lane, lane ^ (1 << bit)) for lane in range(count)])


def rows_swapped(block, bit):
    return jnp.concatenate([block, swap_lane(block, bit)], axis=0)


def gate(value, *others):
    count = len(others)

    def kernel(*refs):
        del refs

    anywhere = pl.BlockSpec(memory_space=pl.ANY)
    return pl.pallas_call(
        kernel,
        in_specs=[anywhere] * (count + 1),
        out_specs=anywhere,
        out_shape=jax.ShapeDtypeStruct(value.shape, value.dtype),
        input_output_aliases={0: 0},
        cost_estimate=pl.CostEstimate(flops=0, bytes_accessed=0, transcendentals=0),
        name="gate",
    )(value, *others)


def normed_rows(values):
    centred = values - jnp.mean(values, axis=-1, keepdims=True)
    inverse = lax.rsqrt(jnp.mean(centred * centred, axis=-1, keepdims=True) + norm_epsilon)
    return centred * inverse, inverse


def mlp_kernel(
    side_ref,
    token_ref,
    own0_ref,
    own1_ref,
    own2_ref,
    other0_ref,
    other1_ref,
    other2_ref,
    own_proj_ref,
    other_proj_ref,
    fc_ref,
    out_ref,
    norm_ref,
    bias_ref,
    grad_ref,
    mid_ref,
    in_ref,
    act_ref,
    hidden_grad_ref,
    back_ref,
    part_ref,
    sum_ref,
    back_acc,
    part_acc,
):
    step = pl.program_id(0)

    @pl.when(step == 0)
    def _():
        is_low = side_ref[0] == 0
        own, other = own_proj_ref[...], other_proj_ref[...]
        proj = jnp.concatenate(
            [jnp.where(is_low, own, other), jnp.where(is_low, other, own)], axis=1
        )
        own = jnp.concatenate([own0_ref[...], own1_ref[...], own2_ref[...]], axis=1)
        other = jnp.concatenate([other0_ref[...], other1_ref[...], other2_ref[...]], axis=1)
        mixed = jnp.concatenate(
            [jnp.where(is_low, own, other), jnp.where(is_low, other, own)], axis=1
        )
        mid = token_ref[...].astype(f32) + (product(mixed, proj, NT) + norm_ref[4:5, :])
        mid_ref[...] = mid
        normed, inverse = normed_rows(mid)
        in_ref[...] = (normed * norm_ref[2:3, :] + norm_ref[3:4, :]).astype(bf16)

    fc_part, out_part = fc_ref[...], out_ref[...]
    values = product(in_ref[...], fc_part) + bias_ref[...]
    square = values * values
    curve = jnp.tanh(gelu_scale * (values + 0.044715 * values * square))
    gate_up = 0.5 * (1.0 + curve)
    act = (values * gate_up).astype(bf16)
    act_ref[...] = act
    slope = gate_up + (0.5 * gelu_scale) * values * (1.0 - curve * curve) * (
        1.0 + (3.0 * 0.044715) * square
    )
    hidden_grad = (product(grad_ref[...], out_part) * slope).astype(bf16)
    hidden_grad_ref[...] = hidden_grad
    sum_ref[...] = jnp.sum(hidden_grad.astype(f32), axis=0, keepdims=True)
    back = product(hidden_grad, fc_part, NT)
    part = product(act, out_part, NT)

    @pl.when(step == 0)
    def _():
        back_acc[...] = back
        part_acc[...] = part

    @pl.when(step > 0)
    def _():
        back_acc[...] += back
        part_acc[...] += part

    @pl.when(step == pl.num_programs(0) - 1)
    def _():
        back_ref[...] = back_acc[...].astype(bf16)
        part_ref[...] = part_acc[...].astype(bf16)


def mlp(side, tokens, own, other, full, norm_rows, hidden_bias, grads, chunk, chunks):
    rows, width = tokens.shape
    hidden = hidden_bias.shape[1]
    half = PAIR * len(own)
    part_rows = rows // chunks
    steps = 3
    span = hidden // steps

    def tall(columns):
        return pl.BlockSpec((part_rows, columns), lambda step: (chunk, 0))

    def fixed(shape, column=0):
        return pl.BlockSpec(shape, lambda step: (0, column))

    def moving(size, first=0):
        return pl.BlockSpec((size, span), lambda step: (0, first + step))

    return pl.pallas_call(
        mlp_kernel,
        grid=(steps,),
        in_specs=[pl.BlockSpec(memory_space=pltpu.SMEM), tall(width)]
        + [tall(PAIR)] * 6
        + [
            fixed((width, half), 2 * hidden // half),
            fixed((width, half), full.shape[1] // half - 1),
            moving(width),
            moving(width, steps),
            fixed((6, width)),
            moving(1),
            tall(width),
        ],
        out_specs=[
            fixed((part_rows, width)),
            fixed((part_rows, width)),
            moving(part_rows),
            moving(part_rows),
            fixed((part_rows, width)),
            fixed((part_rows, width)),
            moving(1),
        ],
        out_shape=[
            jax.ShapeDtypeStruct((part_rows, width), f32),
            jax.ShapeDtypeStruct((part_rows, width), bf16),
            jax.ShapeDtypeStruct((part_rows, hidden), bf16),
            jax.ShapeDtypeStruct((part_rows, hidden), bf16),
            jax.ShapeDtypeStruct((part_rows, width), bf16),
            jax.ShapeDtypeStruct((part_rows, width), bf16),
            jax.ShapeDtypeStruct((1, hidden), f32),
        ],
        scratch_shapes=[pltpu.VMEM((part_rows, width), f32), pltpu.VMEM((part_rows, width), f32)],
        compiler_params=pltpu.CompilerParams(vmem_limit_bytes=60 << 20),
        cost_estimate=pl.CostEstimate(
            flops=10 * part_rows * width * hidden,
            bytes_accessed=4 * width * hidden + 20 * part_rows * width,
            transcendentals=part_rows * hidden,
        ),
        name="mlp",
    )(side, tokens, *own, *other, full, full, full, full, norm_rows, hidden_bias, grads)


def weight_kernel(in0_ref, in1_ref, grad_ref, hidden0_ref, hidden1_ref, act0_ref, act1_ref, made_ref, turned_ref):
    step = pl.program_id(0)
    half = pl.num_programs(0) // 2
    rows = in0_ref.shape[0]

    @pl.when(step == 0)
    def _():
        turned_ref[:, :rows] = in0_ref[...].T
        turned_ref[:, rows:] = in1_ref[...].T

    @pl.when(step == half)
    def _():
        turned_ref[...] = grad_ref[...].T

    @pl.when(step < half)
    def _():
        made_ref[...] = product(
            turned_ref[...], jnp.concatenate([hidden0_ref[...], hidden1_ref[...]], axis=0)
        ).astype(bf16)

    @pl.when(step >= half)
    def _():
        made_ref[...] = product(
            turned_ref[...], jnp.concatenate([act0_ref[...], act1_ref[...]], axis=0)
        ).astype(bf16)


def weight_grads(mlp_in, grads, hidden_grad, act):
    rows, width = mlp_in[0].shape
    hidden = act[0].shape[1]
    span = hidden // 3
    whole = pl.BlockSpec((rows, width), lambda step: (0, 0))
    early = pl.BlockSpec((rows, span), lambda step: (0, jnp.minimum(step, 2)))
    late = pl.BlockSpec((rows, span), lambda step: (0, jnp.maximum(step - 3, 0)))
    return pl.pallas_call(
        weight_kernel,
        grid=(6,),
        in_specs=[whole, whole, pl.BlockSpec((2 * rows, width), lambda step: (0, 0))]
        + [early] * 2
        + [late] * 2,
        out_specs=pl.BlockSpec((width, span), lambda step: (0, step)),
        out_shape=jax.ShapeDtypeStruct((width, 2 * hidden), bf16),
        scratch_shapes=[pltpu.VMEM((width, 2 * rows), bf16)],
        compiler_params=pltpu.CompilerParams(vmem_limit_bytes=60 << 20),
        cost_estimate=pl.CostEstimate(
            flops=8 * rows * width * hidden,
            bytes_accessed=8 * rows * hidden + 4 * width * hidden,
            transcendentals=0,
        ),
        name="weight_grads",
    )(*mlp_in, grads, *hidden_grad, *act)


def middle_kernel(own_ref, other_ref, mid_ref, grad_ref, norm_ref, proj_ref, e1_ref, turned_ref, mixed_ref, sum_ref):
    @pl.when(pl.program_id(0) == 0)
    def _():
        sum_ref[...] = jnp.zeros_like(sum_ref)

    back = own_ref[...].astype(f32) + other_ref[...].astype(f32)
    grad = grad_ref[...].astype(f32)
    normed, inverse = normed_rows(mid_ref[...])
    scaled = back * norm_ref[2:3, :]
    inner = jnp.mean(scaled, axis=-1, keepdims=True)
    cross = jnp.mean(scaled * normed, axis=-1, keepdims=True)
    e1 = grad + inverse * (scaled - inner - normed * cross)
    e1_ref[...] = e1
    low = e1.astype(bf16)
    turned_ref[...] = low.T
    mixed_ref[...] = product(low, proj_ref[...]).astype(bf16)
    for row, term in enumerate((back * normed, back, e1, grad)):
        sum_ref[row : row + 1, :] += jnp.sum(term, axis=0, keepdims=True)


def middle(own, other, mid, grads, norm_rows, full, half, chunk):
    rows, width = own.shape
    tile = min(TILE, rows)
    steps = rows // tile
    column = full.shape[1] // half - 2
    plain = pl.BlockSpec((tile, width), lambda step: (step, 0))
    return pl.pallas_call(
        middle_kernel,
        grid=(steps,),
        in_specs=[
            plain,
            plain,
            plain,
            pl.BlockSpec((tile, width), lambda step: (chunk * steps + step, 0)),
            pl.BlockSpec((6, width), lambda step: (0, 0)),
            pl.BlockSpec((width, half), lambda step: (0, column)),
        ],
        out_specs=[
            plain,
            pl.BlockSpec((width, tile), lambda step: (0, step)),
            pl.BlockSpec((tile, half), lambda step: (step, 0)),
            pl.BlockSpec((4, width), lambda step: (0, 0)),
        ],
        out_shape=[
            jax.ShapeDtypeStruct((rows, width), f32),
            jax.ShapeDtypeStruct((width, rows), bf16),
            jax.ShapeDtypeStruct((rows, half), bf16),
            jax.ShapeDtypeStruct((4, width), f32),
        ],
        compiler_params=pltpu.CompilerParams(vmem_limit_bytes=60 << 20),
        cost_estimate=pl.CostEstimate(
            flops=2 * rows * width * half, bytes_accessed=18 * rows * width, transcendentals=0
        ),
        name="middle",
    )(own, other, mid, grads, norm_rows, full)


def bank_rows(kind, bank):
    if kind == 0:
        return bank.transpose(0, 2, 1, 3)
    return bank if kind == 2 else jnp.swapaxes(bank, 1, 2)


def rows_of(kind, ref, slot=0):
    if kind == 0:
        return jnp.concatenate([ref[slot, part] for part in range(3)], axis=1)
    return ref[slot]


def pack_kernel(tie_ref, *refs, scale, padded, kinds):
    del tie_ref
    *bank_refs, made_ref = refs
    at = 0
    for kind, ref in zip(kinds, bank_refs):
        rows = rows_of(kind, ref) * scale
        width = rows.shape[1]
        if padded:
            made_ref[kind] = jnp.zeros(made_ref.shape[1:], made_ref.dtype)
            made_ref[kind, :, :width] = rows.astype(made_ref.dtype)
        else:
            made_ref[:, at : at + width] = rows.astype(made_ref.dtype)
        at += width


def pack(tie_sources, banks, other, scale, kind_of, padded=0, kinds=PACKED):
    def spec(kind):
        param = matrix_params[kind]

        def index(step, tie_ref):
            slot = tie_ref[param]
            return (1 - slot if other else slot,) + (0,) * (banks[kind].ndim - 1)

        return pl.BlockSpec((1,) + banks[kind].shape[1:], index)

    shard_rows = banks[0].shape[2]
    width = sum(banks[kind][0].size // shard_rows for kind in kinds)
    shape = (KINDS, shard_rows, padded) if padded else (shard_rows, width)
    return pl.pallas_call(
        functools.partial(pack_kernel, scale=scale, padded=padded, kinds=kinds),
        grid_spec=pltpu.PrefetchScalarGridSpec(
            num_scalar_prefetch=1,
            grid=(1,),
            in_specs=[spec(kind) for kind in kinds],
            out_specs=pl.BlockSpec(shape, lambda step, tie_ref: (0,) * len(shape)),
        ),
        out_shape=jax.ShapeDtypeStruct(shape, kind_of),
        compiler_params=pltpu.CompilerParams(vmem_limit_bytes=60 << 20),
        cost_estimate=pl.CostEstimate(
            flops=0, bytes_accessed=16 * shard_rows * width, transcendentals=0
        ),
        name="pack",
    )(tie_sources, *[banks[kind] for kind in kinds])


def collect_kernel(first_ref, low_ref, high_ref, triple_ref, hidden0_ref, hidden1_ref, made_ref):
    width = made_ref.shape[1]
    half = triple_ref.shape[2]
    made_ref[0:2, :] = first_ref[...]
    made_ref[2:6, :] = low_ref[...] + high_ref[...]
    made_ref[6:7, :half] = jnp.sum(triple_ref[0].astype(f32), axis=0, keepdims=True)
    made_ref[6:7, half:] = jnp.sum(triple_ref[2].astype(f32), axis=0, keepdims=True)
    for row in range(2):
        span = slice(row * width, (row + 1) * width)
        made_ref[7 + row : 8 + row, :] = hidden0_ref[:, span] + hidden1_ref[:, span]


def collect(*terms):
    width = terms[0].shape[1]
    return pl.pallas_call(
        collect_kernel,
        in_specs=[pl.BlockSpec(memory_space=pltpu.VMEM)] * len(terms),
        out_specs=pl.BlockSpec(memory_space=pltpu.VMEM),
        out_shape=jax.ShapeDtypeStruct((9, width), f32),
        compiler_params=pltpu.CompilerParams(vmem_limit_bytes=60 << 20),
        cost_estimate=pl.CostEstimate(flops=0, bytes_accessed=2 * terms[3].size, transcendentals=0),
        name="collect",
    )(*terms)


def momentum_kernel(reduced_ref, second_ref, decayed_ref, rows_ref, sent_ref, *, half, pairs):
    hidden = sent_ref.shape[2]
    reduced = reduced_ref[0].astype(f32)
    for plane in range(1, KINDS):
        reduced += reduced_ref[plane].astype(f32)
    ordered = [
        reduced[:, (4 * pair + part) * PAIR : (4 * pair + part + 1) * PAIR]
        for part in (3, 0, 1, 2)
        for pair in range(pairs)
    ]
    first = jnp.concatenate(ordered, axis=1)
    rows_ref[:, : 2 * hidden] = decayed_ref[:, : 2 * hidden] + second_ref[...].astype(f32)
    rows_ref[:, 2 * hidden :] = decayed_ref[:, 2 * hidden :] + first
    sent_ref[...] = jnp.zeros_like(sent_ref)
    sent_ref[2] = rows_ref[:, :hidden].astype(bf16)
    sent_ref[3] = rows_ref[:, hidden : 2 * hidden].astype(bf16)
    sent_ref[1, :, :half] = rows_ref[:, 2 * hidden : 2 * hidden + half].astype(bf16)
    sent_ref[0, :, : 3 * half] = rows_ref[:, 2 * hidden + half :].astype(bf16)


def new_momentum(reduced, second, decayed, half):
    shard_rows, width = decayed.shape
    hidden = second.shape[1] // 2
    return pl.pallas_call(
        functools.partial(momentum_kernel, half=half, pairs=half // PAIR),
        in_specs=[pl.BlockSpec(memory_space=pltpu.VMEM)] * 3,
        out_specs=[pl.BlockSpec(memory_space=pltpu.VMEM)] * 2,
        out_shape=[
            jax.ShapeDtypeStruct((shard_rows, width), f32),
            jax.ShapeDtypeStruct((KINDS, shard_rows, hidden), bf16),
        ],
        compiler_params=pltpu.CompilerParams(vmem_limit_bytes=60 << 20),
        cost_estimate=pl.CostEstimate(
            flops=0, bytes_accessed=16 * shard_rows * width, transcendentals=0
        ),
        name="new_momentum",
    )(reduced, second, decayed)


def input_grad_kernel(triple_ref, weight_ref, made_ref):
    grads = jnp.concatenate([triple_ref[0], triple_ref[1], triple_ref[2]], axis=1)
    made_ref[...] = product(grads, weight_ref[...], NT).astype(bf16)


def input_grads(triple_grad, full):
    kinds, rows, half = triple_grad.shape
    width = full.shape[0]
    tile = min(2 * TILE, rows)
    return pl.pallas_call(
        input_grad_kernel,
        grid=(rows // tile,),
        in_specs=[
            pl.BlockSpec((kinds, tile, half), lambda step: (0, step, 0)),
            pl.BlockSpec((width, kinds * half), lambda step: (0, 0)),
        ],
        out_specs=pl.BlockSpec((tile, width), lambda step: (step, 0)),
        out_shape=jax.ShapeDtypeStruct((rows, width), bf16),
        compiler_params=pltpu.CompilerParams(vmem_limit_bytes=60 << 20),
        cost_estimate=pl.CostEstimate(
            flops=2 * rows * width * kinds * half, bytes_accessed=8 * rows * width, transcendentals=0
        ),
        name="input_grads",
    )(triple_grad, full)


def finish_kernel(
    token_ref,
    first_ref,
    other_first_ref,
    mid_ref,
    part_ref,
    other_part_ref,
    e1_ref,
    norm_ref,
    *refs,
):
    out_ref, grad_ref, sum_ref = refs[-3:]

    @pl.when(pl.program_id(0) == 0)
    def _():
        sum_ref[...] = jnp.zeros_like(sum_ref)

    out_ref[...] = (
        mid_ref[...]
        + (part_ref[...].astype(f32) + other_part_ref[...].astype(f32) + norm_ref[5:6, :])
    ).astype(bf16)
    back = first_ref[...].astype(f32) + other_first_ref[...].astype(f32)
    normed, inverse = normed_rows(token_ref[...].astype(f32))
    scaled = back * norm_ref[0:1, :]
    inner = jnp.mean(scaled, axis=-1, keepdims=True)
    cross = jnp.mean(scaled * normed, axis=-1, keepdims=True)
    grad_ref[...] = (e1_ref[...] + inverse * (scaled - inner - normed * cross)).astype(bf16)
    for row, term in enumerate((back * normed, back)):
        sum_ref[row : row + 1, :] += jnp.sum(term, axis=0, keepdims=True)


def finish(tokens, first, other_first, mids, parts, other_parts, e1, norm_rows):
    rows, width = tokens.shape
    half = rows // 2
    tile = min(TILE, half)
    steps = half // tile

    def whole(chunk):
        return pl.BlockSpec((tile, width), lambda step: (chunk * steps + step, 0))

    plain = pl.BlockSpec((tile, width), lambda step: (step, 0))
    made, sums = [], []
    for chunk in range(2):
        *made, total = pl.pallas_call(
            finish_kernel,
            grid=(steps,),
            in_specs=[whole(chunk)] * 3
            + [plain] * 4
            + [pl.BlockSpec((6, width), lambda step: (0, 0))]
            + [pl.BlockSpec(memory_space=pl.ANY)] * len(made),
            out_specs=[
                whole(chunk),
                whole(chunk),
                pl.BlockSpec((2, width), lambda step: (0, 0)),
            ],
            out_shape=[
                jax.ShapeDtypeStruct((rows, width), bf16),
                jax.ShapeDtypeStruct((rows, width), bf16),
                jax.ShapeDtypeStruct((2, width), f32),
            ],
            input_output_aliases={8: 0, 9: 1} if made else {},
            compiler_params=pltpu.CompilerParams(vmem_limit_bytes=60 << 20),
            cost_estimate=pl.CostEstimate(
                flops=40 * half * width, bytes_accessed=22 * half * width, transcendentals=0
            ),
            name="finish",
        )(
            tokens,
            first,
            other_first,
            mids[chunk],
            parts[chunk],
            other_parts[chunk],
            e1[chunk],
            norm_rows,
            *made,
        )
        sums.append(total)
    return (*made, sums[0] + sums[1])


def put_rows(kind, ref, slot, rows):
    if kind == 0:
        half = ref.shape[3]
        for part in range(3):
            ref[slot, part] = rows[:, part * half : (part + 1) * half]
    else:
        ref[slot] = rows


def momentum_out_kernel(tie_ref, rows_ref, *refs):
    at = 0
    for kind, bank_ref, made_ref in zip(PACKED, refs[:KINDS], refs[KINDS:]):
        width = bank_ref[0].size // rows_ref.shape[0]
        renewed = rows_ref[:, at : at + width]
        at += width
        for slot in range(bank_ref.shape[0]):
            chosen = tie_ref[matrix_params[kind]] == slot

            @pl.when(chosen)
            def _():
                put_rows(kind, made_ref, slot, renewed)

            @pl.when(jnp.logical_not(chosen))
            def _():
                made_ref[slot] = matrix_decay * bank_ref[slot]


def weight_out_kernel(tie_ref, chosen_ref, kept_ref, *refs):
    weight_refs, average_refs = refs[:KINDS], refs[KINDS : 2 * KINDS]
    new_refs, mean_refs = refs[2 * KINDS : 3 * KINDS], refs[3 * KINDS :]
    for kind in range(KINDS):
        width = weight_refs[kind][0].size // chosen_ref.shape[1]
        for slot in range(weight_refs[kind].shape[0]):
            chosen = tie_ref[matrix_params[kind]] == slot
            rows = jnp.where(chosen, chosen_ref[kind, :, :width], kept_ref[kind, :, :width])
            step = (-update_factors[kind]) * rows.astype(f32)
            new = rows_of(kind, weight_refs[kind], slot) + step
            put_rows(kind, new_refs[kind], slot, new)
            mean = average_decay * rows_of(kind, average_refs[kind], slot)
            put_rows(kind, mean_refs[kind], slot, mean + (1.0 - average_decay) * new)


def out_call(kernel, tie_sources, operands, banks, name):
    inside = pl.BlockSpec(memory_space=pltpu.VMEM)
    size = sum(bank.size for bank in banks)
    return pl.pallas_call(
        kernel,
        in_specs=[pl.BlockSpec(memory_space=pltpu.SMEM)] + [inside] * len(operands),
        out_specs=[inside] * len(banks),
        out_shape=[jax.ShapeDtypeStruct(bank.shape, f32) for bank in banks],
        compiler_params=pltpu.CompilerParams(vmem_limit_bytes=60 << 20),
        cost_estimate=pl.CostEstimate(flops=0, bytes_accessed=12 * size, transcendentals=0),
        name=name,
    )(tie_sources, *operands)


def arrange_kernel(*refs, count):
    *pieces, out_ref = refs
    plane, lane = lax.axis_index("plane"), lax.axis_index("lane")
    for flip, piece in enumerate(pieces):
        for shift in range(KINDS):
            out_ref[lax.rem(plane + KINDS - shift, KINDS) * count + (lane ^ flip)] = piece[shift]


def dp_gather(rows, *sooner):
    count = lax.axis_size("lane")
    size, width = rows.shape
    if size % 16:
        made = lax.all_gather(rows, DP, axis=0, tiled=True)
        return made
    planes = jnp.stack(
            [rows]
            + [
                lax.ppermute(
                    rows, "plane", [(plane, (plane + shift) % KINDS) for plane in range(KINDS)]
                )
                for shift in range(1, KINDS)
            ]
    )
    pieces = [planes]
    order = [0]
    for bit in reversed(range(count.bit_length() - 1)):
        if bit == 0:
            pieces[-1] = gate(pieces[-1], *sooner)
        pieces += [swap_lane(piece, bit) for piece in pieces]
        order += [flip | (1 << bit) for flip in order]
    pieces = [piece for unused_flip, piece in sorted(zip(order, pieces), key=lambda pair: pair[0])]
    made = pl.pallas_call(
        functools.partial(arrange_kernel, count=count),
        in_specs=[pl.BlockSpec(memory_space=pltpu.VMEM)] * count,
        out_specs=pl.BlockSpec(memory_space=pltpu.VMEM),
        out_shape=jax.ShapeDtypeStruct((KINDS * count, size, width), bf16),
        compiler_params=pltpu.CompilerParams(vmem_limit_bytes=60 << 20),
        cost_estimate=pl.CostEstimate(
            flops=0, bytes_accessed=4 * KINDS * count * size * width, transcendentals=0
        ),
        name="arrange",
    )(*pieces)
    return made.reshape(KINDS * count * size, width)


def axis_sum(terms, axis):
    count = lax.axis_size(axis)

    def swapped(flip):
        return lax.ppermute(terms, axis, [(place, place ^ flip) for place in range(count)])

    for bit in range(2, count.bit_length() - 1):
        terms = terms + swapped(1 << bit)
    return (terms + swapped(1)) + (swapped(2) + swapped(3))


def lane_reduce(kept, sent):
    shard_rows, width = kept.shape[1:]
    lane = lax.axis_index("lane")
    lane_bits = lax.axis_size("lane").bit_length() - 1
    stages = []
    for bit in range(lane_bits):
        if bit > 0:
            view = part.reshape(-1, 2, shard_rows, width)
            own_bit = (lane >> bit) & 1
            kept = lax.dynamic_index_in_dim(view, own_bit, 1, keepdims=False)
            sent = lax.dynamic_index_in_dim(view, 1 - own_bit, 1, keepdims=False)
        part = (kept.astype(f32) + swap_lane(sent, bit).astype(f32)).astype(bf16)
        stages.append(part)
    return part.reshape(KINDS, shard_rows, width), stages


def plane_rows(outgoing):
    arrived = lax.all_to_all(outgoing, "plane", split_axis=0, concat_axis=0, tiled=True)
    return arrived.reshape(-1, outgoing.shape[2])


def plane_gather(block, waits=(), last=()):
    lane_bits = lax.axis_size("lane").bit_length() - 1
    if waits and waits[0]:
        block = gate(block, *waits[0])
    for bit in range(2, lane_bits):
        block = rows_swapped(block, bit)
    middle = block.shape[1] // 2
    low, high = block[:, :middle], block[:, middle:]
    low_other, high_other = swap_lane(low, 1), swap_tensor(high)
    if waits:
        low_other, high_other = gate(low_other, *waits[1]), gate(high_other, *waits[1])
    low = jnp.stack([low, low_other])
    high = jnp.stack([high, high_other])
    mine = [low, swap_tensor(low), high, swap_lane(high, 1)]
    if last:
        mine[3] = gate(mine[3], *last)
    return mine + [swap_lane(piece, 0) for piece in mine]


def returned(own, shard_rows):
    own = own[: KINDS * shard_rows].reshape(KINDS, shard_rows, -1)
    return lax.all_to_all(own, "plane", split_axis=0, concat_axis=0, tiled=True)


def per_device(
    tokens,
    cotangent,
    tie_sources,
    attn_weight,
    attn_momentum,
    attn_average,
    proj_weight,
    proj_momentum,
    proj_average,
    fc_weight,
    fc_momentum,
    fc_average,
    out_weight,
    out_momentum,
    out_average,
    norm_vectors,
    norm_momentum,
    head_bias,
    head_bias_momentum,
    fc_bias,
    fc_bias_momentum,
):
    row_count, model_width = tokens.shape
    dp_count = lax.axis_size("plane") * lax.axis_size("lane")
    shard_rows = model_width // dp_count
    half_width = proj_weight.shape[1]
    hidden_half = fc_weight.shape[2]
    widths = (3 * half_width, half_width, hidden_half, hidden_half)
    slot_count = attn_weight.shape[0]

    def choose_slot(bank, param_index):
        return lax.dynamic_index_in_dim(bank, tie_sources[param_index], 0, keepdims=False)

    weight_banks, momentum_banks, average_banks = (
        [bank_rows(kind, bank) for kind, bank in enumerate(banks)]
        for banks in (
            (attn_weight, proj_weight, fc_weight, out_weight),
            (attn_momentum, proj_momentum, fc_momentum, out_momentum),
            (attn_average, proj_average, fc_average, out_average),
        )
    )
    norm_rows = jnp.stack(
        [
            norm_vectors[tie_sources[param_index], row_index]
            for row_index, param_index in enumerate(row_params)
        ]
    )

    attn_rows = pack(tie_sources, weight_banks, False, 1.0, bf16, kinds=PACKED[3:])
    low_rows = pack(tie_sources, weight_banks, False, 1.0, bf16, kinds=PACKED[:3])
    inputs = tokens.astype(f32)
    attn_normed, unused_unit, unused_inverse = layer_norm(inputs, norm_rows[0], norm_rows[1])
    attn_in = attn_normed.astype(bf16)
    turned_in = attn_in.T
    decayed_rows = pack(tie_sources, momentum_banks, False, matrix_decay, f32)
    kept_out = pack(tie_sources, momentum_banks, True, matrix_decay, bf16, hidden_half)
    attn_full = dp_gather(attn_rows, turned_in, decayed_rows, kept_out)
    other_proj_rows = swap_tensor(low_rows[:, 2 * hidden_half :])
    full = lax.all_gather(
        jnp.concatenate([low_rows, other_proj_rows], axis=1),
        DP,
        axis=0,
        tiled=True,
    )
    pairs = half_width // PAIR

    query_bias = choose_slot(head_bias, 3)
    hidden_bias = choose_slot(fc_bias, 9)
    projected = jnp.dot(attn_in, attn_full, preferred_element_type=f32)
    bias_row = jnp.concatenate([query_bias[0], jnp.zeros_like(query_bias[0]), query_bias[1]])
    triple = (projected + bias_row[None]).astype(bf16)
    own_mixed, other_mixed, log_totals = [], [], []
    for pair in range(pairs):
        mixed, totals = attend(triple, pair, pairs)
        own_mixed.append(mixed)
        other_mixed.append(swap_tensor(mixed))
        log_totals.append(totals)

    side = lax.axis_index("tensor").astype(jnp.int32).reshape(1)
    chunk_rows = norm_rows
    made = []
    for chunk in range(2):
        made.append(
            mlp(
                side,
                tokens,
                own_mixed,
                other_mixed,
                full,
                chunk_rows,
                hidden_bias[None],
                cotangent,
                chunk,
                2,
            )
        )
        chunk_rows = gate(norm_rows, made[0][4])
    mids, mlp_in, act, hidden_grad, backs, parts, hidden_terms = zip(*made)
    other_backs = [swap_tensor(back) for back in backs]
    kept_rows = plane_rows(gate(kept_out, backs[1]))
    middles = []
    for chunk in range(2):
        own_back = backs[chunk]
        if chunk == 1:
            second_part = weight_grads(
                (gate(mlp_in[0], middles[0][0]), mlp_in[1]), cotangent, hidden_grad, act
            )
            own_back = gate(own_back, second_part, kept_rows)
        middles.append(
            middle(
                own_back,
                other_backs[chunk],
                mids[chunk],
                cotangent,
                norm_rows,
                full,
                half_width,
                chunk,
            )
        )
    e1, turned_mid, mixed_grad, middle_terms = zip(*middles)
    second_shard = lax.psum_scatter(second_part, DP, scatter_dimension=0, tiled=True)
    other_parts = [swap_tensor(gate(part, *mixed_grad)) for part in parts]
    kept_pieces = plane_gather(kept_rows, [(second_part,), mixed_grad])
    triple_grad, attn_kept, attn_sent = attend_back(
        triple,
        (mixed_grad[0], mixed_grad[1]),
        log_totals,
        turned_in,
        turned_mid,
        own_mixed,
        pairs,
        shard_rows,
    )
    part, stages = lane_reduce(
        attn_kept, gate(attn_sent, kept_pieces[1], kept_pieces[3], other_parts[0])
    )
    first_part = input_grads(triple_grad, attn_full)
    other_first = swap_tensor(first_part)
    whole_shape = (model_width, 2 * hidden_half)
    own_shape = (-(-KINDS * shard_rows // 16) * 16, hidden_half)
    kept_whole = newton_call(
        first_kernel,
        [gate(kept_pieces[0], stages[0])] + kept_pieces[1:],
        whole_shape,
        *whole_shape,
        8,
    )
    first_shard = lax.all_to_all(
        gate(part, kept_whole, *other_parts), "plane", split_axis=0, concat_axis=0, tiled=True
    )
    kept_own = newton_call(
        last_kernel, [gate(kept_whole, stages[-1])], own_shape, *whole_shape, 4
    )
    renewed_rows, outgoing = new_momentum(
        gate(first_shard, other_first, kept_own), second_shard, decayed_rows, half_width
    )
    chosen_rows = plane_rows(outgoing)
    block_output, input_grad, norm_one_terms = finish(
        tokens,
        first_part,
        other_first,
        mids,
        parts,
        other_parts,
        e1,
        gate(norm_rows, renewed_rows),
    )
    collected = collect(norm_one_terms, *middle_terms, triple_grad, *hidden_terms)
    lane_terms = axis_sum(collected, "lane")
    terms = axis_sum(lane_terms, "plane")
    ordered = [momentum_banks[kind] for kind in PACKED]
    new_moments = out_call(
        momentum_out_kernel,
        tie_sources,
        [gate(renewed_rows, lane_terms)] + ordered,
        ordered,
        "momentum_out",
    )
    kept_updates = returned(gate(kept_own, chosen_rows), shard_rows)
    chosen_pieces = plane_gather(
        gate(chosen_rows, collected),
        [(), (lane_terms,)],
        [terms, kept_updates, *new_moments],
    )
    new_moments = [new_moments[PACKED.index(kind)] for kind in range(KINDS)]
    norm_grad = terms[:6]
    bias_grad = terms[6].reshape(2, half_width)
    fc_bias_grad = terms[7:].reshape(hidden_half)

    slot_ids = jnp.arange(slot_count, dtype=jnp.int32)
    rate = 0.1 / math.sqrt(row_count * dp_count)
    norm_ties = jnp.stack([tie_sources[param_index] for param_index in row_params])
    norm_bank_grad = jnp.where(
        slot_ids[:, None, None] == norm_ties[None, :, None], norm_grad[None], 0.0
    )
    head_bank_grad = jnp.where((slot_ids == tie_sources[3])[:, None, None], bias_grad[None], 0.0)
    hidden_bank_grad = jnp.where((slot_ids == tie_sources[9])[:, None], fc_bias_grad[None], 0.0)
    new_norm_momentum = vector_decay * norm_momentum + norm_bank_grad
    new_norm_vectors = norm_vectors - rate * new_norm_momentum
    new_head_bias_momentum = vector_decay * head_bias_momentum + head_bank_grad
    new_head_bias = head_bias - rate * new_head_bias_momentum
    new_fc_bias_momentum = vector_decay * fc_bias_momentum + hidden_bank_grad
    new_fc_bias = fc_bias - rate * new_fc_bias_momentum

    chosen_own = newton_call(
        all_kernel,
        [gate(chosen_pieces[0], block_output)]
        + chosen_pieces[1:],
        own_shape,
        *whole_shape,
        14,
        [pltpu.VMEM(whole_shape, bf16)],
    )
    chosen_updates = returned(chosen_own, shard_rows)
    made = out_call(
        weight_out_kernel,
        tie_sources,
        [chosen_updates, kept_updates, *weight_banks, *average_banks],
        weight_banks + average_banks,
        "weight_out",
    )
    results = []
    for kind in range(KINDS):
        results += [
            bank_rows(kind, bank)
            for bank in (made[kind], new_moments[kind], made[KINDS + kind])
        ]
    return (
        block_output,
        input_grad,
        *results,
        new_norm_vectors,
        new_norm_momentum,
        new_head_bias,
        new_head_bias_momentum,
        new_fc_bias,
        new_fc_bias_momentum,
    )


def solution(mesh):
    dp_count, tensor_count = mesh.devices.shape
    grid = Mesh(
        mesh.devices.reshape(KINDS, dp_count // KINDS, tensor_count), ("plane", "lane", "tensor")
    )
    token_spec = P(DP, None)
    attn_spec = P(None, DP, None, "tensor")
    side_spec = P(None, "tensor", DP)
    fc_spec = P(None, DP, "tensor")
    bank_specs = (attn_spec,) * 3 + (side_spec,) * 3 + (fc_spec,) * 3 + (side_spec,) * 3
    vector_specs = (P(),) * 2 + (P(None, None, "tensor"),) * 2 + (P(None, "tensor"),) * 2
    return jax.shard_map(
        per_device,
        mesh=grid,
        in_specs=(token_spec, token_spec, P()) + bank_specs + vector_specs,
        out_specs=(token_spec, token_spec) + bank_specs + vector_specs,
        check_vma=False,
    )
```
